256 devices in a mesh: bead: 16 (over z_lo, y), space: 16 (over x, z_hi, core).
Axes of the slice: x: 4, y: 4, z: 8 (z_hi: 2, z_lo: 4; z = z_hi * 4 + z_lo), core: 2. Of those that a mesh axis runs over, the one named last changes fastest.
Arguments:
- positions: float32 [32, 3, 4096], P('bead', None, 'space'), may hold values from -6 to 6
- momenta: float32 [32, 3, 4096], P('bead', None, 'space'), may hold values from -12 to 12
- species: int32 [4096], P('space'), may hold values 0 or 1
- neighbours: int32 [128, 4096], P(None, 'space'), may hold values from 0 to 512, as said below
- ghost_index: int32 [2, 2048], P(None, 'space'), may hold values from 0 to 255, as said below
- sparse_points: float32 [64, 512], replicated, may hold values from -6 to 6
- coefficients: float32 [2, 512], replicated, may hold values from -6 to 6
- noise: float32 [32, 6, 4096], P('bead', None, 'space'), may hold values from -6 to 6
Outputs:
- new_positions: float32 [32, 3, 4096], P('bead', None, 'space')
- new_momenta: float32 [32, 3, 4096], P('bead', None, 'space')
- forces: float32 [32, 3, 4096], P('bead', None, 'space')
The draws below stay inside these ranges and needn't reach their ends.
Inputs may be any that keep to these rules, and one draw needn't show every extreme that they name: A column lists an atom's neighbours as indices into its slab's table: 0 to 255 own atoms, then 128 atoms from the slab below, then 128 from the slab above; 512 marks padding, which follows the real entries. An atom never lists itself. An atom in its slab's lower face list references only own atoms and atoms from below, one in the upper face list only own atoms and atoms from above. Every atom has 64 or more real entries, and some atom of every slab has 128. `ghost_index`: columns s * 128 to (s + 1) * 128 - 1 belong to slab s and hold indices of its own atoms, 0 to 255; the two rows of a slab together name each of its atoms once.
All inputs are finite; a program needn't handle non-finite values. No bound on the sum of `species` on one device may be relied on, other than what follows from the above.
Results may differ from the reference program's by a relative error of at most 0.0003.
Values sent between devices are 32-bit elements; how exact they have to be, the bound alone decides.
No kernel may reach another device: no remote copies, remote signals or barrier semaphores. Data moves between devices by JAX's collectives and lax.ppermute only.
A program may use at most 64 MiB of HBM per device.

```python
import math
import jax
import jax.numpy as jnp
from jax import lax

BEADS = 32
ATOM_DEV = 256
GHOST = 128
ATOMS = 4096
NBR = 128
DESC = 64
SPARSE = 512
N_SPACE = 16


def face_orders(key):
    slabs = ATOMS // ATOM_DEV
    keys = jax.random.split(jax.random.fold_in(key, 11), slabs)
    return jax.vmap(lambda one: jax.random.permutation(one, ATOM_DEV))(keys).astype(jnp.int32)


def draw_ghost_index(key, part):
    orders = face_orders(key)
    lower = orders[:, :GHOST].reshape(-1)
    upper = orders[:, GHOST:2 * GHOST].reshape(-1)
    return jnp.stack([lower, upper]).astype(jnp.int32)


def draw_neighbours(key, part):
    orders = face_orders(key)
    key = jax.random.fold_in(key, 5)
    slabs = ATOMS // ATOM_DEV
    width = ATOM_DEV + 2 * GHOST

    def one_slab(order, slab_key):
        keys = jax.random.split(slab_key, 4)
        atom = jnp.arange(ATOM_DEV, dtype=jnp.int32)
        side = jnp.full((ATOM_DEV,), 2, jnp.int32).at[order[:GHOST]].set(0).at[order[GHOST:2 * GHOST]].set(1)
        offset = jax.random.randint(keys[0], (NBR, ATOM_DEV), 1, ATOM_DEV)
        own = (atom[None, :] + offset) % ATOM_DEV
        remote = ATOM_DEV + side[None, :] * GHOST + jax.random.randint(keys[1], (NBR, ATOM_DEV), 0, GHOST)
        pick = jax.random.randint(keys[2], (NBR, ATOM_DEV), 0, 4)
        entry = jnp.where((pick == 0) & (side[None, :] < 2), remote, own)
        filled = jax.random.randint(keys[3], (ATOM_DEV,), NBR // 2, NBR + 1)
        filled = jnp.where(atom == order[ATOM_DEV - 1], NBR, filled)
        slot = jnp.arange(NBR, dtype=jnp.int32)[:, None]
        return jnp.where(slot < filled[None, :], entry, width).astype(jnp.int32)
    lists = jax.vmap(one_slab)(orders, jax.random.split(key, slabs))
    return jnp.transpose(lists, (1, 0, 2)).reshape(NBR, ATOMS).astype(jnp.int32)


def touch_ends(array, stream_key, least, top_value):
    longest = array.shape.index(max(array.shape))
    spots = []
    for shift in (0, 1):
        where = [jax.random.randint(jax.random.fold_in(stream_key, axis), (), 0, length) for axis, length in enumerate(array.shape)]
        where[longest] = (where[longest] + shift) % array.shape[longest]
        spots.append(tuple(where))
    return array.at[spots[0]].set(least).at[spots[1]].set(top_value)


def steps_of(own_key, extent, cuts, least, largest):
    loudness = 1.0
    for dim, parts in cuts:
        heights = jax.random.uniform(jax.random.fold_in(jax.random.fold_in(own_key, 6), dim), (parts,), jnp.float32, least / len(cuts), largest / len(cuts))
        loudness = loudness * jnp.repeat(jnp.exp(heights), extent[dim] // parts).reshape((-1,) + (1,) * (len(extent) - 1 - dim))
    return loudness


def normal_values(key, extent, scale, reach, cuts=(), kind=jnp.bfloat16):
    entries = scale * jax.random.normal(key, extent, jnp.float32)
    if cuts:
        entries = entries * steps_of(key, extent, cuts, -0.22, 0.18)
    return jnp.clip(entries, -reach, reach).astype(kind)


def setup_inputs(seed: int = 0) -> dict:
    splits = jax.random.split(jax.random.key(seed), 9)
    positions = normal_values(splits[0], (BEADS, 3, ATOMS), 1.0, 6.0, ((0, 16), (2, 16)), jnp.float32)
    momenta = normal_values(splits[1], (BEADS, 3, ATOMS), 2.0, 12.0, ((0, 16), (2, 16)), jnp.float32)
    species = touch_ends((jax.random.randint(splits[2], (ATOMS,), 0, 3) < 2).astype(jnp.int32), jax.random.fold_in(splits[2], 1), 0, 1)
    neighbours = draw_neighbours(jax.random.fold_in(splits[8], 71), 0)
    ghost_index = draw_ghost_index(jax.random.fold_in(splits[8], 71), 0)
    sparse_points = normal_values(splits[5], (DESC, SPARSE), 1.0, 6.0, (), jnp.float32)
    coefficients = normal_values(splits[6], (2, SPARSE), 1.0, 6.0, (), jnp.float32)
    noise = normal_values(splits[7], (BEADS, 6, ATOMS), 1.0, 6.0, ((0, 16), (2, 16)), jnp.float32)
    return {"positions": positions, "momenta": momenta, "species": species, "neighbours": neighbours, "ghost_index": ghost_index, "sparse_points": sparse_points, "coefficients": coefficients, "noise": noise}


cutoff = 5.0
soften = 0.25
time_step = 0.5
kick = 0.25
friction = 0.2
epsilon = 1e-06
oxygen_mass = 16.0
hydrogen_mass = 1.0

def normalize_columns(matrix):
    return matrix / jnp.sqrt(lax.optimization_barrier(jnp.sum(matrix * matrix, axis=0, keepdims=True)) + epsilon)

def table_gradient(table, spec_table, neighbours, basis, coefficients):
    size = neighbours.shape[1]
    width = table.shape[1] - 1
    block = math.gcd(size, 512)
    nrad = basis.shape[0] // 2
    centers = cutoff * jnp.arange(nrad, dtype=jnp.float32) / nrad
    sharp = nrad * nrad / (2.0 * cutoff * cutoff)

    def energy(tab, start):
        links = lax.dynamic_slice_in_dim(neighbours, start, block, 1)
        live = (links < width).astype(jnp.float32)
        safe = jnp.minimum(links, width)
        near = tab[:, safe]
        own = lax.dynamic_slice_in_dim(tab, start, block, 1)
        delta = near - own[:, None, :]
        dist = jnp.sqrt(lax.optimization_barrier(jnp.sum(delta * delta, axis=0)) + soften)
        ratio = dist * dist / (cutoff * cutoff)
        smooth = jnp.where(dist < cutoff, (1.0 - ratio) ** 2, 0.0) * live
        hydro = spec_table[safe]
        radial = jnp.exp(-sharp * (dist[None] - centers[:, None, None]) ** 2) * smooth[None]
        part_o = lax.optimization_barrier(jnp.sum(radial * (1.0 - hydro)[None], axis=1))
        part_h = lax.optimization_barrier(jnp.sum(radial * hydro[None], axis=1))
        desc = jnp.concatenate([part_o, part_h], axis=0)
        unit = normalize_columns(desc)
        intersection = lax.dot_general(basis, unit, (((0,), (0,)), ((), ())), precision=lax.Precision.HIGHEST, preferred_element_type=jnp.float32)
        kind = lax.dynamic_slice_in_dim(spec_table, start, block, 0)
        weight = coefficients[0][:, None] * (1.0 - kind)[None] + coefficients[1][:, None] * kind[None]
        return jnp.sum(weight * intersection * intersection)

    def advance(total, start):
        return (total + jax.grad(energy)(table, start), None)
    starts = jnp.arange(size // block, dtype=jnp.int32) * block
    total, _ = lax.scan(advance, jnp.zeros_like(table), starts)
    return total

def mode_tables(count):
    index = jnp.arange(count, dtype=jnp.int32)
    phase = (index[:, None] * index[None, :] % count).astype(jnp.float32) * (2.0 * math.pi / count)
    column = index[None, :]
    scale = math.sqrt(2.0 / count)
    flat = 1.0 / math.sqrt(count)
    cmat = jnp.where(column == 0, flat, jnp.where(2 * column < count, scale * jnp.cos(phase), jnp.where(2 * column == count, flat * jnp.cos(phase), scale * jnp.sin(phase))))
    freq = 2.0 * jnp.sin(index.astype(jnp.float32) * (math.pi / count))
    damping = jnp.where(index == 0, friction, 2.0 * freq)
    return (cmat.astype(jnp.float32), freq.astype(jnp.float32), damping.astype(jnp.float32))

def evolve(modes, noise, freq, damping, mass):
    freq = freq[:, None, None]
    keep = jnp.exp(-kick * damping)[:, None, None]
    fresh = jnp.sqrt(1.0 - keep * keep)
    weight = mass[None, None, :]
    amplitude = jnp.sqrt(weight)
    place = modes[:, 0:3]
    moment = keep * modes[:, 3:6] + fresh * amplitude * noise[:, 0:3]
    cosine = jnp.cos(time_step * freq)
    sine = jnp.sin(time_step * freq)
    spread = jnp.where(freq > 0, sine / jnp.where(freq > 0, freq, 1.0), time_step)
    place_new = cosine * place + spread * moment / weight
    moment = cosine * moment - weight * freq * sine * place
    moment = keep * moment + fresh * amplitude * noise[:, 3:6]
    return jnp.concatenate([place_new, moment], axis=1)

def reference(positions, momenta, species, neighbours, ghost_index, sparse_points, coefficients, noise):
    kind = species.astype(jnp.float32)
    lists = ghost_index.reshape(2, N_SPACE, GHOST)
    links = jnp.transpose(neighbours.reshape(NBR, N_SPACE, ATOM_DEV), (1, 0, 2))
    basis = normalize_columns(sparse_points)

    def bead_forces(place):
        carried = jnp.concatenate([place, kind[None, :]], axis=0)
        carried = jnp.transpose(carried.reshape(4, N_SPACE, ATOM_DEV), (1, 0, 2))
        lower_face = jax.vmap(lambda rows, picks: rows[:, picks])(carried, lists[0])
        upper_face = jax.vmap(lambda rows, picks: rows[:, picks])(carried, lists[1])
        below = jnp.roll(upper_face, 1, axis=0)
        above = jnp.roll(lower_face, -1, axis=0)
        tables = jnp.concatenate([carried, below, above, jnp.zeros((N_SPACE, 4, 1), jnp.float32)], axis=2)
        grads = lax.map(lambda pair: table_gradient(pair[0][0:3], pair[0][3], pair[1], basis, coefficients), (tables, links))
        own = grads[:, :, :ATOM_DEV]
        to_lower = jnp.roll(grads[:, :, ATOM_DEV:ATOM_DEV + GHOST], -1, axis=0)
        to_upper = jnp.roll(grads[:, :, ATOM_DEV + GHOST:ATOM_DEV + 2 * GHOST], 1, axis=0)
        own = jax.vmap(lambda mine, first, second, upper, lower: mine.at[:, first].add(upper).at[:, second].add(lower))(own, lists[0], lists[1], to_upper, to_lower)
        return -jnp.transpose(own, (1, 0, 2)).reshape(3, ATOMS)
    forces = lax.map(bead_forces, positions)
    half = momenta + kick * forces
    state = jnp.concatenate([positions, half], axis=1)
    cmat, freq, damping = mode_tables(BEADS)
    masses = jnp.where(species > 0, hydrogen_mass, oxygen_mass).astype(jnp.float32)
    modes = jnp.einsum('bk,bra->kra', cmat, state, precision=lax.Precision.HIGHEST)
    moved = evolve(modes, noise, freq, damping, masses)
    result = jnp.einsum('bk,kra->bra', cmat, moved, precision=lax.Precision.HIGHEST)
    return (result[:, 0:3], result[:, 3:6], forces)
```

```python
import functools
import math

import jax
import jax.numpy as jnp
import numpy as np
from jax import lax
from jax.experimental import pallas as pl
from jax.experimental.pallas import tpu as pltpu
from jax.sharding import PartitionSpec as P

BEADS = 32
NRAD = 32
HI = lax.Precision.HIGHEST
F32 = jnp.float32
BF16 = jnp.bfloat16
WHOLE = pl.BlockSpec(memory_space=pltpu.VMEM)


def step_tables():
    index = np.arange(BEADS)
    angle = 2.0 * np.pi * np.outer(index, index) / BEADS
    modes = np.where(
        index == 0,
        1.0 / np.sqrt(BEADS),
        np.where(
            2 * index < BEADS,
            np.sqrt(2.0 / BEADS) * np.cos(angle),
            np.where(
                2 * index == BEADS,
                np.cos(angle) / np.sqrt(BEADS),
                np.sqrt(2.0 / BEADS) * np.sin(angle),
            ),
        ),
    )
    freq = 2.0 * np.sin(np.pi * index / BEADS)
    keep = np.exp(-0.25 * np.where(index == 0, 0.2, 2.0 * freq))
    fresh = np.sqrt(1.0 - keep * keep)
    cosine, sine = np.cos(0.5 * freq), np.sin(0.5 * freq)
    spread = np.where(index == 0, 0.5, sine / np.where(index == 0, 1.0, freq))
    kinds = [
        (0, (modes * cosine) @ modes.T),
        (1, -(modes * (keep * freq * sine)) @ modes.T),
        (0, (modes * (spread * keep)) @ modes.T),
        (1, (modes * (keep * keep * cosine)) @ modes.T),
        (0, modes * (spread * fresh)),
        (1, modes * (keep * cosine * fresh)),
        (1, modes * fresh),
    ]
    base = np.zeros((16, 16, 2, 2, 3, 2, 2, 7, 8))
    for kind, (output, matrix) in enumerate(kinds):
        blocks = matrix.reshape(16, 2, 16, 2)
        for sender in range(16):
            for half in range(2):
                for b in range(2):
                    for c in range(3):
                        base[sender, :, half, output, c, :, half, kind, c * 2 + b] = blocks[
                            :, :, sender, b
                        ]
    return base.reshape(16, 384, 112).astype(np.float32)


STEP_TABLE = step_tables()


def lanes(row, count=8):
    return jnp.broadcast_to(row, (count, 128))


def take(chunk, index):
    return jnp.take_along_axis(chunk, index, axis=1, mode="promise_in_bounds")


def take_pair(low, high, index):
    local = index & 127
    return jnp.where(index < 128, take(low, local), take(high, local))


def halves(pieces):
    return jnp.concatenate([p[:, 0:128] for p in pieces] + [p[:, 128:256] for p in pieces], axis=0)


def fetch_all(sources, targets, semaphores):
    copies = [
        pltpu.make_async_copy(source, target, semaphores.at[i])
        for i, (source, target) in enumerate(zip(sources, targets))
    ]
    for copy in copies:
        copy.start()
    for copy in copies:
        copy.wait()


def pack_kernel(positions_hbm, species_hbm, ghost_hbm, out_ref, positions, species, ghost, sems):
    fetch_all((positions_hbm, species_hbm, ghost_hbm), (positions, species, ghost), sems)
    out_ref[...] = jnp.concatenate(
        [positions[c] for c in range(3)]
        + [species[...].astype(F32)]
        + [jnp.concatenate([ghost[0:1, :], ghost[1:2, :]], axis=1).astype(F32)],
        axis=0,
    )


def split(value):
    coarse = value.astype(BF16)
    return coarse, (value - coarse.astype(F32)).astype(BF16)


def dot3(left, right):
    a, b = split(left)
    c, d = split(right)
    dot = functools.partial(jnp.dot, preferred_element_type=F32)
    return dot(a, c) + (dot(a, d) + dot(b, c))


def odd_slab():
    return jnp.full((8, 128), lax.axis_index("space") % 2, jnp.int32) == 1


def column_sums(values):
    row = lax.broadcasted_iota(jnp.int32, (8, 128), 0)
    top = row < 4
    four = [
        jnp.where(top, values[k], values[k + 4])
        + pltpu.roll(jnp.where(top, values[k + 4], values[k]), 4, 0)
        for k in range(4)
    ]
    top = (row & 3) < 2
    two = [
        jnp.where(
            top, four[k] + pltpu.roll(four[k], 6, 0), four[k + 2] + pltpu.roll(four[k + 2], 2, 0)
        )
        for k in range(2)
    ]
    top = (row & 1) < 1
    return jnp.where(top, two[0] + pltpu.roll(two[0], 7, 0), two[1] + pltpu.roll(two[1], 1, 0))


def taps():
    away = (lax.broadcasted_iota(jnp.int32, (8, 128), 0) - 4).astype(F32)
    return jnp.exp(away * away * -0.5)


def quad_kernel(sparse_ref, coef_ref, quad_ref):
    sparse = sparse_ref[...]
    basis = sparse * lax.rsqrt(jnp.sum(sparse * sparse, axis=0, keepdims=True) + 1e-6)
    scaled = jnp.concatenate([basis * coef_ref[0:1, :], basis * coef_ref[1:2, :]], axis=0)
    quad_ref[...] = lax.dot_general(
        scaled, basis, (((1,), (1,)), ((), ())), precision=HI, preferred_element_type=F32
    )


def scatter(slots, hot_of, value_of):
    return lax.dot_general(
        jnp.concatenate([hot_of(slot) for slot in range(slots)], axis=1),
        jnp.concatenate([value_of(slot) for slot in range(slots)], axis=1),
        (((1,), (1,)), ((), ())),
        preferred_element_type=F32,
    ).T


def levels(count, wide):
    return lax.broadcasted_iota(jnp.int32, (count, wide), 0).astype(F32).astype(BF16)


def one_hot(row, level):
    count, wide = level.shape
    entry = jnp.broadcast_to(row, (16, wide)).astype(BF16)
    one = jnp.ones((16, wide), BF16)
    return jnp.concatenate(
        [
            jnp.where(entry == level[r * 16 : r * 16 + 16], one, jnp.zeros_like(one))
            for r in range(count // 16)
        ],
        axis=0,
    )


def coded(full, row, codes):
    wide = full.shape[1]
    coarse = full.astype(BF16).astype(F32)
    two = jnp.concatenate([coarse, full - coarse], axis=0).astype(BF16)
    code = jnp.broadcast_to(row, (16, wide)).astype(BF16)
    return jnp.concatenate(
        [
            jnp.where(code == jnp.full((16, wide), c, BF16), two, jnp.zeros_like(two))
            for c in range(codes)
        ],
        axis=0,
    )


def joined(sums):
    grad = jnp.concatenate([sums[0:8] + sums[8:16], sums[16:24] + sums[24:32]], axis=1)
    return jnp.where(lax.broadcasted_iota(jnp.int32, grad.shape, 0) < 6, grad, 0.0)


def force_kernel(
    own_ref,
    far_ref,
    close_ref,
    nbr_ref,
    quad_ref,
    to_far_ref,
    to_near_ref,
    grad_ref,
    v_ref,
    index_ref,
    central_ref,
    low_ref,
    code_ref,
    src_ref,
    hyd_ref,
    t_ref,
    geo_ref,
    e_ref,
    p_ref,
    desc_ref,
    g_ref,
):
    odd = odd_slab()

    far = far_ref[...]
    close = close_ref[...]
    far_low, far_high = (lanes(far[7:8, h * 128 : h * 128 + 128]) for h in range(2))
    close_low, close_high = (lanes(close[7:8, h * 128 : h * 128 + 128]) for h in range(2))
    far_pick = jnp.where(odd, far_low, far_high).astype(jnp.int32)
    close_pick = jnp.where(odd, close_high, close_low).astype(jnp.int32)
    far = take_pair(far[:, 0:128], far[:, 128:256], far_pick)
    close = take_pair(close[:, 0:128], close[:, 128:256], close_pick)
    own = own_ref[...]
    listed = own[7:8].astype(jnp.int32)
    chunks = [
        own[:, 0:128],
        own[:, 128:256],
        jnp.where(odd, close, far),
        jnp.where(odd, far, close),
    ]
    for c in range(4):
        for r in range(7):
            src_ref[c * 7 + r] = lanes(chunks[c][r : r + 1])

    for half in range(2):
        cols = slice(half * 128, half * 128 + 128)
        pick = lanes(listed[:, cols])
        central_ref[:, cols] = take_pair(chunks[0], chunks[1], pick)

        def gather(s, carry, half=half, cols=cols, pick=pick):
            rows = pl.ds(pl.multiple_of(s * 8, 8), 8)
            index = take_pair(nbr_ref[rows, 0:128], nbr_ref[rows, 128:256], pick)
            index_ref[half, rows, :] = index
            local = index & 127
            first = index < 128
            own = index < 256
            live = index < 512
            low_ref[half, rows, :] = (index & 63).astype(F32)
            code_ref[half, rows, :] = jnp.where(live & ~own, local >> 6, 2).astype(F32)

            def fetch(r):
                mine = jnp.where(first, take(src_ref[r], local), take(src_ref[7 + r], local))
                return jnp.where(own, mine, take(src_ref[14 + half * 7 + r], local))

            hyd_ref[half, rows, :] = fetch(6)
            for b in range(2):
                bl = b * 2 + half
                delta = [
                    fetch(c * 2 + b) - lanes(central_ref[c * 2 + b : c * 2 + b + 1, cols])
                    for c in range(3)
                ]
                square = delta[0] * delta[0] + delta[1] * delta[1] + delta[2] * delta[2] + 0.25
                inverse = lax.rsqrt(square)
                ratio = square * (1.0 / 25.0)
                keep = jnp.where(live & (ratio < 1.0), 1.0 - ratio, 0.0)
                reach = jnp.minimum(square * inverse * 6.4, 32.0)
                t_ref[bl, rows, :] = reach
                for c in range(3):
                    geo_ref[bl, c, rows, :] = delta[c]
                geo_ref[bl, 3, rows, :] = inverse
                geo_ref[bl, 4, rows, :] = keep
                e_ref[bl, 0, rows, :] = jnp.exp(reach)
                e_ref[bl, 1, rows, :] = jnp.exp(-reach)
            return carry

        lax.fori_loop(0, 16, gather, 0, unroll=16)

    tap = taps()

    def radial(bl, carry):
        half = bl & 1
        for a in range(4):
            center = 8.0 * a + 4.0

            def step(s, total, center=center, a=a):
                rows = pl.ds(pl.multiple_of(s * 8, 8), 8)
                tau = t_ref[bl, rows, :] - center
                keep = geo_ref[bl, 4, rows, :]
                hydro = hyd_ref[half, rows, :]
                up = e_ref[bl, 0, rows, :] * math.exp(-center)
                down = e_ref[bl, 1, rows, :] * math.exp(center)
                tower = [None] * 8
                tower[4] = jnp.exp(tau * tau * -0.5) * (keep * keep)
                for m in range(5, 8):
                    tower[m] = tower[m - 1] * up
                for m in range(3, -1, -1):
                    tower[m] = tower[m + 1] * down
                new = []
                for m in range(8):
                    p_ref[bl, a * 8 + m, rows, :] = tower[m]
                    new.append(total[2 * m] + tower[m])
                    new.append(total[2 * m + 1] + tower[m] * hydro)
                return tuple(new)

            zero = jnp.zeros((8, 128), F32)
            total = lax.fori_loop(0, 16, step, (zero,) * 16, unroll=16)
            every = column_sums(total[0::2])
            hydrogen = column_sums(total[1::2])
            desc_ref[bl, a * 8 : a * 8 + 8, :] = (every - hydrogen) * tap
            desc_ref[bl, NRAD + a * 8 : NRAD + a * 8 + 8, :] = hydrogen * tap
        return carry

    lax.fori_loop(0, 4, radial, 0, unroll=4)

    desc = [desc_ref[bl] for bl in range(4)]
    norm = [lax.rsqrt(jnp.sum(d * d, axis=0, keepdims=True) + 1e-6) for d in desc]
    unit = [d * n for d, n in zip(desc, norm)]
    turned = dot3(quad_ref[...], jnp.concatenate(unit, axis=1))
    tap = jnp.concatenate([taps()] * 8, axis=0)
    for bl in range(4):
        half = bl & 1
        heavy = central_ref[6:7, half * 128 : half * 128 + 128] < 0.5
        mine = turned[:, bl * 128 : bl * 128 + 128]
        slope = jnp.where(heavy, mine[0:64], mine[64:128])
        along = jnp.sum(slope * unit[bl], axis=0, keepdims=True)
        g_ref[bl] = (2.0 * norm[bl]) * (slope - unit[bl] * along) * tap

    group = 4
    grad_ref[6:8, :] = jnp.zeros((2, 256), F32)
    for b in range(2):
        for half in range(2):
            bl = b * 2 + half

            def back(s, total, b=b, bl=bl, half=half):
                start = pl.multiple_of(s * (8 * group), 8 * group)
                rows = [pl.ds(start + 8 * q, 8) for q in range(group)]
                hydro = [hyd_ref[half, r, :] > 0.5 for r in rows]
                plain = [None] * group
                ramp = [None] * group
                for k in range(NRAD - 1, -1, -1):
                    oxygen = lanes(g_ref[bl, k : k + 1, :])
                    hydrogen = lanes(g_ref[bl, NRAD + k : NRAD + k + 1, :])
                    for q in range(group):
                        x = p_ref[bl, k, rows[q], :] * jnp.where(hydro[q], hydrogen, oxygen)
                        plain[q] = x if k == NRAD - 1 else plain[q] + x
                        ramp[q] = plain[q] if k == NRAD - 1 else ramp[q] + plain[q]
                total = list(total)
                for q in range(group):
                    reach = t_ref[bl, rows[q], :]
                    inverse = geo_ref[bl, 3, rows[q], :]
                    keep = geo_ref[bl, 4, rows[q], :]
                    inside = keep > 0.0
                    fade = jnp.where(inside, (-4.0 / 25.0) / jnp.where(inside, keep, 1.0), 0.0)
                    slope = (reach + 1.0) * plain[q] - ramp[q]
                    pull = plain[q] * fade - 6.4 * slope * inverse
                    for c in range(3):
                        part = pull * geo_ref[bl, c, rows[q], :]
                        total[c] = total[c] + part
                        v_ref[half, pl.ds((start + 8 * q) * 8 + c * 2 + b, 8, stride=8), :] = part
                return tuple(total)

            zero = jnp.zeros((8, 128), F32)
            total = lax.fori_loop(0, 16 // group, back, (zero,) * 3, unroll=4)
            for c in range(3):
                grad_ref[c * 2 + b : c * 2 + b + 1, half * 128 : half * 128 + 128] = -jnp.sum(
                    total[c], axis=0, keepdims=True
                )

    copies = []
    level = levels(64, 128)
    for half in range(2):
        sums = scatter(
            128,
            lambda slot, half=half: one_hot(low_ref[half, pl.ds(slot, 1), :], level),
            lambda slot, half=half: coded(
                v_ref[half, pl.ds(slot * 8, 8), :],
                code_ref[half, pl.ds(slot, 1), :],
                2,
            ),
        )
        copies.append(joined(sums))
    to_far_ref[...] = jnp.where(odd, copies[1], copies[0])
    to_near_ref[...] = jnp.where(odd, copies[0], copies[1])


def push_rows(grad, packet_ref):
    push = grad * -0.25
    mass = jnp.where(packet_ref[6:7, :] > 0.5, 1.0, 16.0)
    none = jnp.zeros((8, 256), F32)
    return halves([none, none, push / mass, push, none, none, none])


def base_rows(own, momenta_ref, noise_ref):
    light = own[6:7] > 0.5
    mass = jnp.where(light, 1.0, 16.0)
    root = jnp.where(light, 1.0, 4.0)
    blank = jnp.zeros((2, 256), F32)
    moment = jnp.concatenate([momenta_ref[c] for c in range(3)] + [blank], axis=0)
    first = jnp.concatenate([noise_ref[c] for c in range(3)] + [blank], axis=0)
    second = jnp.concatenate([noise_ref[3 + c] for c in range(3)] + [blank], axis=0)
    return halves(
        [own, own * mass, moment / mass, moment, first / root, first * root, second * root]
    )


def places(packet_ref):
    listed = packet_ref[7:8, :].astype(jnp.int32)
    same = lax.broadcasted_iota(jnp.int32, (256, 256), 0) == listed
    place = lax.broadcasted_iota(jnp.int32, (8, 256), 1).astype(F32).astype(BF16)
    return lax.dot_general(
        place,
        jnp.where(same, 1.0, 0.0).astype(BF16),
        (((1,), (1,)), ((), ())),
        preferred_element_type=F32,
    ).astype(jnp.int32)


def gather_kernel(
    v_ref,
    index_ref,
    grad_ref,
    packet_ref,
    momenta_ref,
    noise_ref,
    table_ref,
    own_ref,
    sum_ref,
    back_ref,
):
    back_ref[...] = places(packet_ref)
    level = levels(128, 256)
    wide = lambda pick, slot: jnp.concatenate([pick(h, slot) for h in range(2)], axis=1)
    index = lambda slot: wide(lambda h, s: index_ref[h, pl.ds(s, 1), :], slot)
    sums = scatter(
        128,
        lambda slot: one_hot((index(slot) & 127).astype(F32), level),
        lambda slot: coded(
            wide(lambda h, s: v_ref[h, pl.ds(s * 8, 8), :], slot),
            (index(slot) >> 7).astype(F32),
            2,
        ),
    )
    passed = joined(sums)
    central = jnp.concatenate(
        [
            take_pair(grad_ref[:, 0:128], grad_ref[:, 128:256], back_ref[:, 0:128]),
            take_pair(grad_ref[:, 0:128], grad_ref[:, 128:256], back_ref[:, 128:256]),
        ],
        axis=1,
    )
    own = passed + central
    own_ref[...] = own
    sum_ref[...] = jnp.dot(
        table_ref[...],
        base_rows(packet_ref[...], momenta_ref, noise_ref) + push_rows(own, packet_ref),
        precision=HI,
        preferred_element_type=F32,
    )


def combine_kernel(
    far_ref, near_ref, back_ref, packet_ref, table_ref, own_ref, base_ref, forces_ref, send_ref
):
    odd = odd_slab()
    low = jnp.where(odd, near_ref[...], far_ref[...])
    high = jnp.where(odd, far_ref[...], near_ref[...])
    passed = jnp.concatenate(
        [take_pair(low, high, back_ref[:, 0:128]), take_pair(low, high, back_ref[:, 128:256])],
        axis=1,
    )
    forces = -own_ref[...] - passed
    for c in range(3):
        forces_ref[c] = forces[c * 2 : c * 2 + 2]
    send_ref[...] = base_ref[...] + dot3(table_ref[...], push_rows(passed, packet_ref))


def finish_kernel(parts_ref, positions_ref, momenta_ref):
    total = parts_ref[0]
    for d in range(1, 16):
        total = total + parts_ref[d]
    for half in range(2):
        cols = slice(half * 128, half * 128 + 128)
        for c in range(3):
            row = half * 12 + c * 2
            positions_ref[c, :, cols] = total[row : row + 2]
            momenta_ref[c, :, cols] = total[row + 6 : row + 8]


def call(kernel, shapes, count, name, mib=1, scratch=(), ints=(), fetched=()):
    buffers = [pltpu.VMEM(shape, F32) for shape in scratch]
    buffers += [pltpu.VMEM(value.shape, value.dtype) for value in fetched]
    if fetched:
        buffers.append(pltpu.SemaphoreType.DMA((len(fetched),)))
    return pl.pallas_call(
        kernel,
        out_shape=[
            jax.ShapeDtypeStruct(shape, jnp.int32 if i in ints else F32)
            for i, shape in enumerate(shapes)
        ],
        in_specs=[WHOLE] * count + [pl.BlockSpec(memory_space=pltpu.HBM)] * len(fetched),
        out_specs=[WHOLE] * len(shapes),
        scratch_shapes=buffers,
        compiler_params=pltpu.CompilerParams(vmem_limit_bytes=mib * 1024 * 1024),
        name=name,
    )


def per_device(
    positions, momenta, species, neighbours, ghost_index, sparse_points, coefficients, noise
):
    size = lax.axis_size("space")
    close = [(i, i ^ 1) for i in range(size)]
    distant = [(i, (i + 1) % size if i % 2 else (i - 1) % size) for i in range(size)]
    turn = lambda value: jnp.transpose(value, (1, 0, 2))
    kind = species.reshape(1, 256)
    own = (turn(positions), kind, ghost_index)
    (packet,) = call(pack_kernel, [(8, 256)], 0, "pack", fetched=own)(*own)
    far = lax.ppermute(packet, "space", distant)
    near = lax.ppermute(packet, "space", close)
    table = lax.dynamic_index_in_dim(
        jnp.asarray(STEP_TABLE), lax.axis_index("bead"), 0, keepdims=False
    )
    (quad,) = call(quad_kernel, [(128, 64)], 2, "quad", 2)(sparse_points, coefficients)
    to_far, to_near, grad, pulls, index = table_gradient(packet, far, near, neighbours, quad)
    from_far = lax.ppermute(to_far, "space", distant)
    from_near = lax.ppermute(to_near, "space", close)
    own_grad, summed, back = call(
        gather_kernel, [(8, 256), (384, 128), (8, 256)], 7, "gather", 8, ints=(2,)
    )(pulls, index, grad, packet, turn(momenta), turn(noise), table)
    forces, send = call(combine_kernel, [(3, 2, 256), (384, 128)], 7, "combine", 4)(
        from_far, from_near, back, packet, table, own_grad, summed
    )
    parts = lax.all_to_all(send.reshape(16, 24, 128), "bead", split_axis=0, concat_axis=0, tiled=True)
    new_positions, new_momenta = call(finish_kernel, [(3, 2, 256)] * 2, 1, "finish")(parts)
    return (turn(new_positions), turn(new_momenta), turn(forces))


def table_gradient(*args):
    return call(
        force_kernel,
        [(8, 128), (8, 128), (8, 256), (2, 1024, 128), (2, 128, 128)],
        5,
        "force",
        20,
        scratch=[
            (8, 256),
            (2, 128, 128),
            (2, 128, 128),
            (28, 8, 128),
            (2, 128, 128),
            (4, 128, 128),
            (4, 5, 128, 128),
            (4, 2, 128, 128),
            (4, 32, 128, 128),
            (4, 64, 128),
            (4, 64, 128),
        ],
        ints=(4,),
    )(*args)


def solution(mesh):
    placed = (
        P("bead", None, "space"),
        P("bead", None, "space"),
        P("space"),
        P(None, "space"),
        P(None, "space"),
        P(),
        P(),
        P("bead", None, "space"),
    )
    return jax.shard_map(
        per_device,
        mesh=mesh,
        in_specs=placed,
        out_specs=(P("bead", None, "space"), P("bead", None, "space"), P("bead", None, "space")),
        check_vma=False,
    )
```

```python
import functools
import math

import jax
import jax.numpy as jnp
import numpy as np
from jax import lax
from jax.experimental import pallas as pl
from jax.experimental.pallas import tpu as pltpu
from jax.sharding import PartitionSpec as P

BEADS = 32
NRAD = 32
HI = lax.Precision.HIGHEST
F32 = jnp.float32
BF16 = jnp.bfloat16
WHOLE = pl.BlockSpec(memory_space=pltpu.VMEM)


def step_tables():
    index = np.arange(BEADS)
    angle = 2.0 * np.pi * np.outer(index, index) / BEADS
    modes = np.where(
        index == 0,
        1.0 / np.sqrt(BEADS),
        np.where(
            2 * index < BEADS,
            np.sqrt(2.0 / BEADS) * np.cos(angle),
            np.where(
                2 * index == BEADS,
                np.cos(angle) / np.sqrt(BEADS),
                np.sqrt(2.0 / BEADS) * np.sin(angle),
            ),
        ),
    )
    freq = 2.0 * np.sin(np.pi * index / BEADS)
    keep = np.exp(-0.25 * np.where(index == 0, 0.2, 2.0 * freq))
    fresh = np.sqrt(1.0 - keep * keep)
    cosine, sine = np.cos(0.5 * freq), np.sin(0.5 * freq)
    spread = np.where(index == 0, 0.5, sine / np.where(index == 0, 1.0, freq))
    kinds = [
        (0, (modes * cosine) @ modes.T),
        (1, -(modes * (keep * freq * sine)) @ modes.T),
        (0, (modes * (spread * keep)) @ modes.T),
        (1, (modes * (keep * keep * cosine)) @ modes.T),
        (0, modes * (spread * fresh)),
        (1, modes * (keep * cosine * fresh)),
        (1, modes * fresh),
    ]
    base = np.zeros((16, 16, 2, 2, 3, 2, 2, 7, 8))
    for kind, (output, matrix) in enumerate(kinds):
        blocks = matrix.reshape(16, 2, 16, 2)
        for sender in range(16):
            for half in range(2):
                for b in range(2):
                    for c in range(3):
                        base[sender, :, half, output, c, :, half, kind, c * 2 + b] = blocks[
                            :, :, sender, b
                        ]
    return base.reshape(16, 384, 112).astype(np.float32)


STEP_TABLE = step_tables()


def lanes(row, count=8):
    return jnp.broadcast_to(row, (count, 128))


def take(chunk, index):
    return jnp.take_along_axis(chunk, index, axis=1, mode="promise_in_bounds")


def take_pair(low, high, index):
    local = index & 127
    return jnp.where(index < 128, take(low, local), take(high, local))


def halves(pieces):
    return jnp.concatenate([p[:, 0:128] for p in pieces] + [p[:, 128:256] for p in pieces], axis=0)


def fetch(sources, targets, semaphores):
    copies = [
        pltpu.make_async_copy(source, target, semaphores.at[i])
        for i, (source, target) in enumerate(zip(sources, targets))
    ]
    for copy in copies:
        copy.start()
    return copies


def pack_kernel(positions_ref, species_ref, ghost_ref, nbr_ref, own_ref, far_ref, near_ref):
    rows = jnp.concatenate(
        [positions_ref[c] for c in range(3)]
        + [species_ref[...].astype(F32)]
        + [jnp.concatenate([ghost_ref[0:1, :], ghost_ref[1:2, :]], axis=1).astype(F32)],
        axis=0,
    )
    odd = odd_slab()
    low, high = (lanes(ghost_ref[h : h + 1, :]) for h in range(2))
    picks = jnp.where(odd, high, low), jnp.where(odd, low, high)
    for half in range(2):
        block = slice(half * 8, half * 8 + 8)
        part = rows[:, half * 128 : half * 128 + 128]
        own_ref[block, :] = part
        far_ref[block, :] = part
        near_ref[block, :] = part
    for s in range(16):
        block = slice(s * 8, s * 8 + 8)
        left, right = nbr_ref[block, 0:128], nbr_ref[block, 128:256]
        for target, pick in zip((far_ref, near_ref), picks):
            target[16 + s * 8 : 24 + s * 8, :] = take_pair(left, right, pick).astype(F32)


def split(value):
    coarse = value.astype(BF16)
    return coarse, (value - coarse.astype(F32)).astype(BF16)


def dot3(left, right):
    a, b = split(left)
    c, d = split(right)
    dot = functools.partial(jnp.dot, preferred_element_type=F32)
    return dot(a, c) + (dot(a, d) + dot(b, c))


def odd_slab():
    return jnp.full((8, 128), lax.axis_index("space") % 2, jnp.int32) == 1


def column_sums(values):
    row = lax.broadcasted_iota(jnp.int32, (8, 128), 0)
    top = row < 4
    four = [
        jnp.where(top, values[k], values[k + 4])
        + pltpu.roll(jnp.where(top, values[k + 4], values[k]), 4, 0)
        for k in range(4)
    ]
    top = (row & 3) < 2
    two = [
        jnp.where(
            top, four[k] + pltpu.roll(four[k], 6, 0), four[k + 2] + pltpu.roll(four[k + 2], 2, 0)
        )
        for k in range(2)
    ]
    top = (row & 1) < 1
    return jnp.where(top, two[0] + pltpu.roll(two[0], 7, 0), two[1] + pltpu.roll(two[1], 1, 0))


def taps():
    away = (lax.broadcasted_iota(jnp.int32, (8, 128), 0) - 4).astype(F32)
    return jnp.exp(away * away * -0.5)


def quadratic(sparse, weight):
    basis = sparse * lax.rsqrt(jnp.sum(sparse * sparse, axis=0, keepdims=True) + 1e-6)
    scaled = jnp.concatenate([basis * weight[0:1], basis * weight[1:2]], axis=0)
    return lax.dot_general(
        scaled, basis, (((1,), (1,)), ((), ())), precision=HI, preferred_element_type=F32
    )


def places(own):
    same = lax.broadcasted_iota(jnp.int32, (256, 256), 0) == own[7:8].astype(jnp.int32)
    place = lax.broadcasted_iota(jnp.int32, (8, 256), 1).astype(F32).astype(BF16)
    return lax.dot_general(
        place,
        jnp.where(same, 1.0, 0.0).astype(BF16),
        (((1,), (1,)), ((), ())),
        preferred_element_type=F32,
    ).astype(jnp.int32)


def scatter(slots, hot_of, value_of):
    return lax.dot_general(
        jnp.concatenate([hot_of(slot) for slot in range(slots)], axis=1),
        jnp.concatenate([value_of(slot) for slot in range(slots)], axis=1),
        (((1,), (1,)), ((), ())),
        preferred_element_type=F32,
    ).T


def levels(count, wide):
    return lax.broadcasted_iota(jnp.int32, (count, wide), 0).astype(F32).astype(BF16)


def one_hot(row, level):
    count, wide = level.shape
    entry = jnp.broadcast_to(row, (16, wide)).astype(BF16)
    one = jnp.ones((16, wide), BF16)
    return jnp.concatenate(
        [
            jnp.where(entry == level[r * 16 : r * 16 + 16], one, jnp.zeros_like(one))
            for r in range(count // 16)
        ],
        axis=0,
    )


def coded(full, row, codes):
    wide = full.shape[1]
    coarse = full.astype(BF16).astype(F32)
    two = jnp.concatenate([coarse, full - coarse], axis=0).astype(BF16)
    code = jnp.broadcast_to(row, (16, wide)).astype(BF16)
    return jnp.concatenate(
        [
            jnp.where(code == jnp.full((16, wide), c, BF16), two, jnp.zeros_like(two))
            for c in range(codes)
        ],
        axis=0,
    )


def joined(sums):
    grad = jnp.concatenate(
        [sums[c : c + 8] + sums[c + 8 : c + 16] for c in range(0, sums.shape[0], 16)], axis=1
    )
    return jnp.where(lax.broadcasted_iota(jnp.int32, grad.shape, 0) < 6, grad, 0.0)


def pair_forces(chunks, picks, index_of, code_of, quad_of, grad_ref, work):
    (v_ref, central_ref, low_ref, code_ref, src_ref, hyd_ref, t_ref, geo_ref, e_ref, p_ref) = work[:10]
    desc_ref, g_ref = work[10:]
    for half in range(2):
        for c in range(3):
            for r in range(7):
                src_ref[(half * 3 + c) * 7 + r] = lanes(chunks[half][c][r : r + 1])

    for half in range(2):
        cols = slice(half * 128, half * 128 + 128)
        central_ref[:, cols] = take_pair(chunks[half][0], chunks[half][1], picks[half])

        def gather(s, carry, half=half, cols=cols):
            rows = pl.ds(pl.multiple_of(s * 8, 8), 8)
            index = index_of(half, rows)
            local = index & 127
            first = index < 128
            own = index < 256
            live = index < 512
            low, code = code_of(index)
            low_ref[half, rows, :] = low.astype(F32)
            code_ref[half, rows, :] = code.astype(F32)

            def fetch(r):
                found = [take(src_ref[(half * 3 + c) * 7 + r], local) for c in range(3)]
                return jnp.where(own, jnp.where(first, found[0], found[1]), found[2])

            hyd_ref[half, rows, :] = fetch(6)
            for b in range(2):
                bl = b * 2 + half
                delta = [
                    fetch(c * 2 + b) - lanes(central_ref[c * 2 + b : c * 2 + b + 1, cols])
                    for c in range(3)
                ]
                square = delta[0] * delta[0] + delta[1] * delta[1] + delta[2] * delta[2] + 0.25
                inverse = lax.rsqrt(square)
                ratio = square * (1.0 / 25.0)
                keep = jnp.where(live & (ratio < 1.0), 1.0 - ratio, 0.0)
                reach = jnp.minimum(square * inverse * 6.4, 32.0)
                t_ref[bl, rows, :] = reach
                for c in range(3):
                    geo_ref[bl, c, rows, :] = delta[c]
                geo_ref[bl, 3, rows, :] = inverse
                geo_ref[bl, 4, rows, :] = keep
                e_ref[bl, 0, rows, :] = jnp.exp(reach)
                e_ref[bl, 1, rows, :] = jnp.exp(-reach)
            return carry

        lax.fori_loop(0, 16, gather, 0, unroll=16)

    tap = taps()

    def radial(bl, carry):
        half = bl & 1
        for a in range(4):
            center = 8.0 * a + 4.0

            def step(s, total, center=center, a=a):
                rows = pl.ds(pl.multiple_of(s * 8, 8), 8)
                tau = t_ref[bl, rows, :] - center
                keep = geo_ref[bl, 4, rows, :]
                hydro = hyd_ref[half, rows, :]
                up = e_ref[bl, 0, rows, :] * math.exp(-center)
                down = e_ref[bl, 1, rows, :] * math.exp(center)
                tower = [None] * 8
                tower[4] = jnp.exp(tau * tau * -0.5) * (keep * keep)
                for m in range(5, 8):
                    tower[m] = tower[m - 1] * up
                for m in range(3, -1, -1):
                    tower[m] = tower[m + 1] * down
                new = []
                for m in range(8):
                    p_ref[bl, a * 8 + m, rows, :] = tower[m]
                    new.append(total[2 * m] + tower[m])
                    new.append(total[2 * m + 1] + tower[m] * hydro)
                return tuple(new)

            zero = jnp.zeros((8, 128), F32)
            total = lax.fori_loop(0, 16, step, (zero,) * 16, unroll=16)
            every = column_sums(total[0::2])
            hydrogen = column_sums(total[1::2])
            desc_ref[bl, a * 8 : a * 8 + 8, :] = (every - hydrogen) * tap
            desc_ref[bl, NRAD + a * 8 : NRAD + a * 8 + 8, :] = hydrogen * tap
        return carry

    lax.fori_loop(0, 4, radial, 0, unroll=4)

    desc = [desc_ref[bl] for bl in range(4)]
    norm = [lax.rsqrt(jnp.sum(d * d, axis=0, keepdims=True) + 1e-6) for d in desc]
    unit = [d * n for d, n in zip(desc, norm)]
    turned = dot3(quad_of(), jnp.concatenate(unit, axis=1))
    tap = jnp.concatenate([taps()] * 8, axis=0)
    for bl in range(4):
        half = bl & 1
        heavy = central_ref[6:7, half * 128 : half * 128 + 128] < 0.5
        mine = turned[:, bl * 128 : bl * 128 + 128]
        slope = jnp.where(heavy, mine[0:64], mine[64:128])
        along = jnp.sum(slope * unit[bl], axis=0, keepdims=True)
        g_ref[bl] = (2.0 * norm[bl]) * (slope - unit[bl] * along) * tap

    group = 4
    if grad_ref is not None:
        grad_ref[6:8, :] = jnp.zeros((2, 256), F32)
    for b in range(2):
        for half in range(2):
            bl = b * 2 + half

            def back(s, total, b=b, bl=bl, half=half):
                start = pl.multiple_of(s * (8 * group), 8 * group)
                rows = [pl.ds(start + 8 * q, 8) for q in range(group)]
                hydro = [hyd_ref[half, r, :] > 0.5 for r in rows]
                plain = [None] * group
                ramp = [None] * group
                for k in range(NRAD - 1, -1, -1):
                    oxygen = lanes(g_ref[bl, k : k + 1, :])
                    hydrogen = lanes(g_ref[bl, NRAD + k : NRAD + k + 1, :])
                    for q in range(group):
                        x = p_ref[bl, k, rows[q], :] * jnp.where(hydro[q], hydrogen, oxygen)
                        plain[q] = x if k == NRAD - 1 else plain[q] + x
                        ramp[q] = plain[q] if k == NRAD - 1 else ramp[q] + plain[q]
                total = list(total)
                for q in range(group):
                    reach = t_ref[bl, rows[q], :]
                    inverse = geo_ref[bl, 3, rows[q], :]
                    keep = geo_ref[bl, 4, rows[q], :]
                    inside = keep > 0.0
                    fade = jnp.where(inside, (-4.0 / 25.0) / jnp.where(inside, keep, 1.0), 0.0)
                    slope = (reach + 1.0) * plain[q] - ramp[q]
                    pull = plain[q] * fade - 6.4 * slope * inverse
                    for c in range(3):
                        part = pull * geo_ref[bl, c, rows[q], :]
                        total[c] = total[c] + part
                        v_ref[half, pl.ds((start + 8 * q) * 8 + c * 2 + b, 8, stride=8), :] = part
                return tuple(total)

            zero = jnp.zeros((8, 128), F32)
            total = lax.fori_loop(0, 16 // group, back, (zero,) * 3, unroll=4)
            for c in range(3):
                if grad_ref is not None:
                    grad_ref[c * 2 + b : c * 2 + b + 1, half * 128 : half * 128 + 128] = -jnp.sum(
                        total[c], axis=0, keepdims=True
                    )


def merged_kernel(
    own_hbm,
    far_hbm,
    near_hbm,
    nbr_hbm,
    sparse_hbm,
    coef_hbm,
    momenta_hbm,
    noise_hbm,
    tables_hbm,
    forces_ref,
    send_ref,
    own_ref,
    far_ref,
    near_ref,
    nbr_ref,
    sparse_ref,
    coef_ref,
    momenta_ref,
    noise_ref,
    table_ref,
    sems,
    quad_ref,
    grad_ref,
    *work,
):
    copies = fetch(
        (own_hbm, far_hbm, near_hbm, nbr_hbm, sparse_hbm, coef_hbm, momenta_hbm, noise_hbm)
        + (tables_hbm.at[lax.axis_index("bead")],),
        (own_ref, far_ref, near_ref, nbr_ref, sparse_ref, coef_ref, momenta_ref, noise_ref)
        + (table_ref,),
        sems,
    )
    for copy in copies[:4]:
        copy.wait()
    odd = odd_slab()
    chunk = lambda ref, h: ref[h * 8 : h * 8 + 8, :]
    own = [chunk(own_ref, h) for h in range(2)]
    far = [chunk(far_ref, h) for h in range(2)]
    near = [chunk(near_ref, h) for h in range(2)]
    below = [jnp.where(odd, n, f) for f, n in zip(far, near)]
    above = [jnp.where(odd, f, n) for f, n in zip(far, near)]
    listed = lambda slab, h: lanes(slab[h][7:8]).astype(jnp.int32)

    def quad_of():
        for copy in copies[4:]:
            copy.wait()
        quad_ref[...] = quadratic(sparse_ref[...], coef_ref[...])
        return quad_ref[...]

    mine = [listed(own, h) for h in range(2)]
    outer = [listed(below, 1), listed(above, 0)]
    copied = [take_pair(*below, outer[0]), take_pair(*above, outer[1])]
    pair_forces(
        [(*own, copied[h]) for h in range(2)],
        mine,
        lambda half, rows: take_pair(nbr_ref[rows, 0:128], nbr_ref[rows, 128:256], mine[half]),
        lambda index: (index & 63, index >> 6),
        quad_of,
        grad_ref,
        work,
    )
    v_ref, _, low_ref, code_ref = work[:4]
    level = levels(64, 256)
    wide = lambda ref, rows: jnp.concatenate([ref[h, rows, :] for h in range(2)], axis=1)
    passed = joined(
        scatter(
            128,
            lambda slot: one_hot(wide(low_ref, pl.ds(slot, 1)), level),
            lambda slot: coded(wide(v_ref, pl.ds(slot * 8, 8)), wide(code_ref, pl.ds(slot, 1)), 4),
        )
    )

    def index_of(half, rows):
        there = pl.ds(16 + rows.start, rows.size)
        f, n = far_ref[there, :], near_ref[there, :]
        found = jnp.where(odd, n, f) if half == 0 else jnp.where(odd, f, n)
        return found.astype(jnp.int32)

    def code_of(index):
        own = (index >= 256) & (index < 512)
        return index & 63, jnp.where(own, (index & 127) >> 6, 2)

    pair_forces(
        [
            (*slab, take_pair(*own, pick))
            for slab, pick in ((below, mine[0]), (above, mine[1]))
        ],
        outer,
        index_of,
        code_of,
        lambda: quad_ref[...],
        None,
        work,
    )
    level = levels(64, 128)
    returned = [
        joined(
            scatter(
                128,
                lambda slot, half=half: one_hot(low_ref[half, pl.ds(slot, 1), :], level),
                lambda slot, half=half: coded(
                    v_ref[half, pl.ds(slot * 8, 8), :], code_ref[half, pl.ds(slot, 1), :], 2
                ),
            )
        )
        for half in range(2)
    ]
    own = jnp.concatenate(own, axis=1)
    back = places(own)
    total = grad_ref[...] + jnp.concatenate(returned, axis=1)
    grad = passed + jnp.concatenate(
        [
            take_pair(total[:, 0:128], total[:, 128:256], back[:, h * 128 : h * 128 + 128])
            for h in range(2)
        ],
        axis=1,
    )
    for c in range(3):
        forces_ref[c] = -grad[c * 2 : c * 2 + 2]
    rows = base_rows(own, momenta_ref, noise_ref) + push_rows(grad, own)
    send_ref[...] = jnp.dot(table_ref[...], rows, precision=HI, preferred_element_type=F32)


WORK = [
    (2, 1024, 128),
    (8, 256),
    (2, 128, 128),
    (2, 128, 128),
    (42, 8, 128),
    (2, 128, 128),
    (4, 128, 128),
    (4, 5, 128, 128),
    (4, 2, 128, 128),
    (4, 32, 128, 128),
    (4, 64, 128),
    (4, 64, 128),
]


def push_rows(grad, own):
    push = grad * -0.25
    mass = jnp.where(own[6:7] > 0.5, 1.0, 16.0)
    none = jnp.zeros((8, 256), F32)
    return halves([none, none, push / mass, push, none, none, none])


def base_rows(own, momenta_ref, noise_ref):
    light = own[6:7] > 0.5
    mass = jnp.where(light, 1.0, 16.0)
    root = jnp.where(light, 1.0, 4.0)
    blank = jnp.zeros((2, 256), F32)
    moment = jnp.concatenate([momenta_ref[c] for c in range(3)] + [blank], axis=0)
    first = jnp.concatenate([noise_ref[c] for c in range(3)] + [blank], axis=0)
    second = jnp.concatenate([noise_ref[3 + c] for c in range(3)] + [blank], axis=0)
    return halves(
        [own, own * mass, moment / mass, moment, first / root, first * root, second * root]
    )


def finish_kernel(parts_ref, positions_ref, momenta_ref):
    total = parts_ref[0]
    for d in range(1, 16):
        total = total + parts_ref[d]
    for half in range(2):
        cols = slice(half * 128, half * 128 + 128)
        for c in range(3):
            row = half * 12 + c * 2
            positions_ref[c, :, cols] = total[row : row + 2]
            momenta_ref[c, :, cols] = total[row + 6 : row + 8]


LIMIT = 62


def call(kernel, shapes, operands, name, mib, fetched=(), scratch=()):
    buffers = [
        pltpu.VMEM(value.shape[1:] if value.shape == STEP_TABLE.shape else value.shape, value.dtype)
        for value in fetched
    ]
    if fetched:
        buffers.append(pltpu.SemaphoreType.DMA((len(fetched),)))
    return pl.pallas_call(
        kernel,
        out_shape=[jax.ShapeDtypeStruct(shape, F32) for shape in shapes],
        in_specs=[WHOLE] * len(operands) + [pl.BlockSpec(memory_space=pl.ANY)] * len(fetched),
        out_specs=[WHOLE] * len(shapes),
        scratch_shapes=buffers + [pltpu.VMEM(shape, F32) for shape in scratch],
        compiler_params=pltpu.CompilerParams(vmem_limit_bytes=mib * 1024 * 1024),
        name=name,
    )(*operands, *fetched)


def per_device(
    positions, momenta, species, neighbours, ghost_index, sparse_points, coefficients, noise
):
    size = lax.axis_size("space")
    close = [(i, i ^ 1) for i in range(size)]
    distant = [(i, (i + 1) % size if i % 2 else (i - 1) % size) for i in range(size)]
    turn = lambda value: jnp.transpose(value, (1, 0, 2))
    own, to_far, to_near = call(
        pack_kernel,
        [(16, 128), (144, 128), (144, 128)],
        (turn(positions), species.reshape(1, 256), ghost_index, neighbours),
        "pack",
        LIMIT,
    )
    far = lax.ppermute(to_far, "space", distant)
    near = lax.ppermute(to_near, "space", close)
    forces, send = call(
        merged_kernel,
        [(3, 2, 256), (384, 128)],
        (),
        "forces",
        LIMIT,
        (own, far, near, neighbours, sparse_points, coefficients, turn(momenta), turn(noise))
        + (jnp.asarray(STEP_TABLE),),
        [(128, 64), (8, 256)] + WORK,
    )
    parts = lax.all_to_all(send.reshape(16, 24, 128), "bead", split_axis=0, concat_axis=0, tiled=True)
    new_positions, new_momenta = call(finish_kernel, [(3, 2, 256)] * 2, (parts,), "finish", 1)
    return (turn(new_positions), turn(new_momenta), turn(forces))


def solution(mesh):
    placed = (
        P("bead", None, "space"),
        P("bead", None, "space"),
        P("space"),
        P(None, "space"),
        P(None, "space"),
        P(),
        P(),
        P("bead", None, "space"),
    )
    return jax.shard_map(
        per_device,
        mesh=mesh,
        in_specs=placed,
        out_specs=(P("bead", None, "space"), P("bead", None, "space"), P("bead", None, "space")),
        check_vma=False,
    )
```

```python
import functools
import math

import jax
import jax.numpy as jnp
import numpy as np
from jax import lax
from jax.experimental import pallas as pl
from jax.experimental.pallas import tpu as pltpu
from jax.sharding import PartitionSpec as P

BEADS = 32
NRAD = 32
HI = lax.Precision.HIGHEST
F32 = jnp.float32
BF16 = jnp.bfloat16
WHOLE = pl.BlockSpec(memory_space=pltpu.VMEM)


def step_tables():
    index = np.arange(BEADS)
    angle = 2.0 * np.pi * np.outer(index, index) / BEADS
    modes = np.where(
        index == 0,
        1.0 / np.sqrt(BEADS),
        np.where(
            2 * index < BEADS,
            np.sqrt(2.0 / BEADS) * np.cos(angle),
            np.where(
                2 * index == BEADS,
                np.cos(angle) / np.sqrt(BEADS),
                np.sqrt(2.0 / BEADS) * np.sin(angle),
            ),
        ),
    )
    freq = 2.0 * np.sin(np.pi * index / BEADS)
    keep = np.exp(-0.25 * np.where(index == 0, 0.2, 2.0 * freq))
    fresh = np.sqrt(1.0 - keep * keep)
    cosine, sine = np.cos(0.5 * freq), np.sin(0.5 * freq)
    spread = np.where(index == 0, 0.5, sine / np.where(index == 0, 1.0, freq))
    kinds = [
        (0, (modes * cosine) @ modes.T),
        (1, -(modes * (keep * freq * sine)) @ modes.T),
        (0, (modes * (spread * keep)) @ modes.T),
        (1, (modes * (keep * keep * cosine)) @ modes.T),
        (0, modes * (spread * fresh)),
        (1, modes * (keep * cosine * fresh)),
        (1, modes * fresh),
    ]
    base = np.zeros((16, 16, 2, 2, 3, 2, 2, 7, 8))
    for kind, (output, matrix) in enumerate(kinds):
        blocks = matrix.reshape(16, 2, 16, 2)
        for sender in range(16):
            for half in range(2):
                for b in range(2):
                    for c in range(3):
                        base[sender, :, half, output, c, :, half, kind, c * 2 + b] = blocks[
                            :, :, sender, b
                        ]
    return base.reshape(16, 384, 112).astype(np.float32)


STEP_TABLE = step_tables()


def lanes(row, count=8):
    return jnp.broadcast_to(row, (count, 128))


def take(chunk, index):
    return jnp.take_along_axis(chunk, index, axis=1, mode="promise_in_bounds")


def take_pair(low, high, index):
    local = index & 127
    return jnp.where(index < 128, take(low, local), take(high, local))


def halves(pieces):
    return jnp.concatenate([p[:, 0:128] for p in pieces] + [p[:, 128:256] for p in pieces], axis=0)


def fetch(sources, targets, semaphores):
    copies = [
        pltpu.make_async_copy(source, target, semaphores.at[i])
        for i, (source, target) in enumerate(zip(sources, targets))
    ]
    for copy in copies:
        copy.start()
    return copies


def pack_kernel(positions_ref, species_ref, ghost_ref, nbr_ref, own_ref, far_ref, near_ref):
    rows = jnp.concatenate(
        [positions_ref[c] for c in range(3)]
        + [species_ref[...].astype(F32)]
        + [jnp.concatenate([ghost_ref[0:1, :], ghost_ref[1:2, :]], axis=1).astype(F32)],
        axis=0,
    )
    odd = odd_slab()
    low, high = (lanes(ghost_ref[h : h + 1, :]) for h in range(2))
    picks = jnp.where(odd, high, low), jnp.where(odd, low, high)
    for half in range(2):
        block = slice(half * 8, half * 8 + 8)
        part = rows[:, half * 128 : half * 128 + 128]
        own_ref[block, :] = part
        far_ref[block, :] = part
        near_ref[block, :] = part
    for s in range(16):
        block = slice(s * 8, s * 8 + 8)
        left, right = nbr_ref[block, 0:128], nbr_ref[block, 128:256]
        for target, pick in zip((far_ref, near_ref), picks):
            target[16 + s * 8 : 24 + s * 8, :] = take_pair(left, right, pick).astype(F32)


def split(value):
    coarse = value.astype(BF16)
    return coarse, (value - coarse.astype(F32)).astype(BF16)


def dot3(left, right):
    a, b = split(left)
    c, d = split(right)
    dot = functools.partial(jnp.dot, preferred_element_type=F32)
    return dot(a, c) + (dot(a, d) + dot(b, c))


def odd_slab():
    return jnp.full((8, 128), lax.axis_index("space") % 2, jnp.int32) == 1


def column_sums(values):
    row = lax.broadcasted_iota(jnp.int32, (8, 128), 0)
    top = row < 4
    four = [
        jnp.where(top, values[k], values[k + 4])
        + pltpu.roll(jnp.where(top, values[k + 4], values[k]), 4, 0)
        for k in range(4)
    ]
    top = (row & 3) < 2
    two = [
        jnp.where(
            top, four[k] + pltpu.roll(four[k], 6, 0), four[k + 2] + pltpu.roll(four[k + 2], 2, 0)
        )
        for k in range(2)
    ]
    top = (row & 1) < 1
    return jnp.where(top, two[0] + pltpu.roll(two[0], 7, 0), two[1] + pltpu.roll(two[1], 1, 0))


def taps():
    away = (lax.broadcasted_iota(jnp.int32, (8, 128), 0) - 4).astype(F32)
    return jnp.exp(away * away * -0.5)


def quadratic(sparse, weight):
    basis = sparse * lax.rsqrt(jnp.sum(sparse * sparse, axis=0, keepdims=True) + 1e-6)
    scaled = jnp.concatenate([basis * weight[0:1], basis * weight[1:2]], axis=0)
    return lax.dot_general(
        scaled, basis, (((1,), (1,)), ((), ())), precision=HI, preferred_element_type=F32
    )


def places(own):
    same = lax.broadcasted_iota(jnp.int32, (256, 256), 0) == own[7:8].astype(jnp.int32)
    place = lax.broadcasted_iota(jnp.int32, (8, 256), 1).astype(F32).astype(BF16)
    return lax.dot_general(
        place,
        jnp.where(same, 1.0, 0.0).astype(BF16),
        (((1,), (1,)), ((), ())),
        preferred_element_type=F32,
    ).astype(jnp.int32)


def scatter(slots, hot_of, value_of):
    return lax.dot_general(
        jnp.concatenate([hot_of(slot) for slot in range(slots)], axis=1),
        jnp.concatenate([value_of(slot) for slot in range(slots)], axis=1),
        (((1,), (1,)), ((), ())),
        preferred_element_type=F32,
    ).T


def levels(count, wide):
    return lax.broadcasted_iota(jnp.int32, (count, wide), 0).astype(F32).astype(BF16)


def one_hot(row, level):
    count, wide = level.shape
    entry = jnp.broadcast_to(row, (16, wide)).astype(BF16)
    one = jnp.ones((16, wide), BF16)
    return jnp.concatenate(
        [
            jnp.where(entry == level[r * 16 : r * 16 + 16], one, jnp.zeros_like(one))
            for r in range(count // 16)
        ],
        axis=0,
    )


def coded(full, row, codes):
    wide = full.shape[1]
    coarse = full.astype(BF16).astype(F32)
    two = jnp.concatenate([coarse, full - coarse], axis=0).astype(BF16)
    code = jnp.broadcast_to(row, (16, wide)).astype(BF16)
    return jnp.concatenate(
        [
            jnp.where(code == jnp.full((16, wide), c, BF16), two, jnp.zeros_like(two))
            for c in range(codes)
        ],
        axis=0,
    )


def joined(sums):
    grad = jnp.concatenate(
        [sums[c : c + 8] + sums[c + 8 : c + 16] for c in range(0, sums.shape[0], 16)], axis=1
    )
    return jnp.where(lax.broadcasted_iota(jnp.int32, grad.shape, 0) < 6, grad, 0.0)


def pair_forces(chunks, picks, index_of, code_of, quad_of, grad_ref, work):
    (v_ref, central_ref, low_ref, code_ref, src_ref, hyd_ref, t_ref, geo_ref, e_ref, p_ref) = work[:10]
    desc_ref, g_ref = work[10:]
    for half in range(2):
        for c in range(3):
            for r in range(7):
                src_ref[(half * 3 + c) * 7 + r] = lanes(chunks[half][c][r : r + 1])

    for half in range(2):
        cols = slice(half * 128, half * 128 + 128)
        central_ref[:, cols] = take_pair(chunks[half][0], chunks[half][1], picks[half])

        def gather(s, carry, half=half, cols=cols):
            rows = pl.ds(pl.multiple_of(s * 8, 8), 8)
            index = index_of(half, rows)
            local = index & 127
            first = index < 128
            own = index < 256
            live = index < 512
            low, code = code_of(index)
            low_ref[half, rows, :] = low.astype(F32)
            code_ref[half, rows, :] = code.astype(F32)

            def fetch(r):
                found = [take(src_ref[(half * 3 + c) * 7 + r], local) for c in range(3)]
                return jnp.where(own, jnp.where(first, found[0], found[1]), found[2])

            hyd_ref[half, rows, :] = fetch(6)
            for b in range(2):
                bl = b * 2 + half
                delta = [
                    fetch(c * 2 + b) - lanes(central_ref[c * 2 + b : c * 2 + b + 1, cols])
                    for c in range(3)
                ]
                square = delta[0] * delta[0] + delta[1] * delta[1] + delta[2] * delta[2] + 0.25
                inverse = lax.rsqrt(square)
                ratio = square * (1.0 / 25.0)
                keep = jnp.where(live & (ratio < 1.0), 1.0 - ratio, 0.0)
                reach = jnp.minimum(square * inverse * 6.4, 32.0)
                t_ref[bl, rows, :] = reach
                for c in range(3):
                    geo_ref[bl, c, rows, :] = delta[c]
                geo_ref[bl, 3, rows, :] = inverse
                geo_ref[bl, 4, rows, :] = keep
                e_ref[bl, 0, rows, :] = jnp.exp(reach)
                e_ref[bl, 1, rows, :] = jnp.exp(-reach)
            return carry

        lax.fori_loop(0, 16, gather, 0, unroll=16)

    yield
    tap = taps()

    def radial(bl, carry):
        half = bl & 1
        for a in range(4):
            center = 8.0 * a + 4.0

            def step(s, total, center=center, a=a):
                rows = pl.ds(pl.multiple_of(s * 8, 8), 8)
                tau = t_ref[bl, rows, :] - center
                keep = geo_ref[bl, 4, rows, :]
                hydro = hyd_ref[half, rows, :]
                up = e_ref[bl, 0, rows, :] * math.exp(-center)
                down = e_ref[bl, 1, rows, :] * math.exp(center)
                tower = [None] * 8
                tower[4] = jnp.exp(tau * tau * -0.5) * (keep * keep)
                for m in range(5, 8):
                    tower[m] = tower[m - 1] * up
                for m in range(3, -1, -1):
                    tower[m] = tower[m + 1] * down
                new = []
                for m in range(8):
                    p_ref[bl, a * 8 + m, rows, :] = tower[m]
                    new.append(total[2 * m] + tower[m])
                    new.append(total[2 * m + 1] + tower[m] * hydro)
                return tuple(new)

            zero = jnp.zeros((8, 128), F32)
            total = lax.fori_loop(0, 16, step, (zero,) * 16, unroll=16)
            every = column_sums(total[0::2])
            hydrogen = column_sums(total[1::2])
            desc_ref[bl, a * 8 : a * 8 + 8, :] = (every - hydrogen) * tap
            desc_ref[bl, NRAD + a * 8 : NRAD + a * 8 + 8, :] = hydrogen * tap
        return carry

    lax.fori_loop(0, 4, radial, 0, unroll=4)

    yield
    desc = [desc_ref[bl] for bl in range(4)]
    norm = [lax.rsqrt(jnp.sum(d * d, axis=0, keepdims=True) + 1e-6) for d in desc]
    unit = [d * n for d, n in zip(desc, norm)]
    turned = dot3(quad_of(), jnp.concatenate(unit, axis=1))
    tap = jnp.concatenate([taps()] * 8, axis=0)
    for bl in range(4):
        half = bl & 1
        heavy = central_ref[6:7, half * 128 : half * 128 + 128] < 0.5
        mine = turned[:, bl * 128 : bl * 128 + 128]
        slope = jnp.where(heavy, mine[0:64], mine[64:128])
        along = jnp.sum(slope * unit[bl], axis=0, keepdims=True)
        g_ref[bl] = (2.0 * norm[bl]) * (slope - unit[bl] * along) * tap

    yield
    group = 4
    if grad_ref is not None:
        grad_ref[6:8, :] = jnp.zeros((2, 256), F32)
    for b in range(2):
        for half in range(2):
            bl = b * 2 + half

            def back(s, total, b=b, bl=bl, half=half):
                start = pl.multiple_of(s * (8 * group), 8 * group)
                rows = [pl.ds(start + 8 * q, 8) for q in range(group)]
                hydro = [hyd_ref[half, r, :] > 0.5 for r in rows]
                plain = [None] * group
                ramp = [None] * group
                for k in range(NRAD - 1, -1, -1):
                    oxygen = lanes(g_ref[bl, k : k + 1, :])
                    hydrogen = lanes(g_ref[bl, NRAD + k : NRAD + k + 1, :])
                    for q in range(group):
                        x = p_ref[bl, k, rows[q], :] * jnp.where(hydro[q], hydrogen, oxygen)
                        plain[q] = x if k == NRAD - 1 else plain[q] + x
                        ramp[q] = plain[q] if k == NRAD - 1 else ramp[q] + plain[q]
                total = list(total)
                for q in range(group):
                    reach = t_ref[bl, rows[q], :]
                    inverse = geo_ref[bl, 3, rows[q], :]
                    keep = geo_ref[bl, 4, rows[q], :]
                    inside = keep > 0.0
                    fade = jnp.where(inside, (-4.0 / 25.0) / jnp.where(inside, keep, 1.0), 0.0)
                    slope = (reach + 1.0) * plain[q] - ramp[q]
                    pull = plain[q] * fade - 6.4 * slope * inverse
                    for c in range(3):
                        part = pull * geo_ref[bl, c, rows[q], :]
                        total[c] = total[c] + part
                        v_ref[half, pl.ds((start + 8 * q) * 8 + c * 2 + b, 8, stride=8), :] = part
                return tuple(total)

            zero = jnp.zeros((8, 128), F32)
            total = lax.fori_loop(0, 16 // group, back, (zero,) * 3, unroll=4)
            for c in range(3):
                if grad_ref is not None:
                    grad_ref[c * 2 + b : c * 2 + b + 1, half * 128 : half * 128 + 128] = -jnp.sum(
                        total[c], axis=0, keepdims=True
                    )


def merged_kernel(
    own_hbm,
    far_hbm,
    near_hbm,
    nbr_hbm,
    sparse_hbm,
    coef_hbm,
    momenta_hbm,
    noise_hbm,
    tables_hbm,
    forces_ref,
    send_ref,
    own_ref,
    far_ref,
    near_ref,
    nbr_ref,
    sparse_ref,
    coef_ref,
    momenta_ref,
    noise_ref,
    table_ref,
    sems,
    quad_ref,
    grad_ref,
    *work,
):
    work, outer_work = work[: len(WORK)], work[len(WORK) :]
    copies = fetch(
        (own_hbm, far_hbm, near_hbm, nbr_hbm, sparse_hbm, coef_hbm, momenta_hbm, noise_hbm)
        + (tables_hbm.at[lax.axis_index("bead")],),
        (own_ref, far_ref, near_ref, nbr_ref, sparse_ref, coef_ref, momenta_ref, noise_ref)
        + (table_ref,),
        sems,
    )
    for copy in copies[:4]:
        copy.wait()
    odd = odd_slab()
    chunk = lambda ref, h: ref[h * 8 : h * 8 + 8, :]
    own = [chunk(own_ref, h) for h in range(2)]
    far = [chunk(far_ref, h) for h in range(2)]
    near = [chunk(near_ref, h) for h in range(2)]
    below = [jnp.where(odd, n, f) for f, n in zip(far, near)]
    above = [jnp.where(odd, f, n) for f, n in zip(far, near)]
    listed = lambda slab, h: lanes(slab[h][7:8]).astype(jnp.int32)

    def quad_of():
        for copy in copies[4:]:
            copy.wait()
        quad_ref[...] = quadratic(sparse_ref[...], coef_ref[...])
        return quad_ref[...]

    mine = [listed(own, h) for h in range(2)]
    outer = [listed(below, 1), listed(above, 0)]
    copied = [take_pair(*below, outer[0]), take_pair(*above, outer[1])]
    inner_pairs = pair_forces(
        [(*own, copied[h]) for h in range(2)],
        mine,
        lambda half, rows: take_pair(nbr_ref[rows, 0:128], nbr_ref[rows, 128:256], mine[half]),
        lambda index: (index & 63, index >> 6),
        quad_of,
        grad_ref,
        work,
    )
    def index_of(half, rows):
        there = pl.ds(16 + rows.start, rows.size)
        f, n = far_ref[there, :], near_ref[there, :]
        found = jnp.where(odd, n, f) if half == 0 else jnp.where(odd, f, n)
        return found.astype(jnp.int32)

    def code_of(index):
        own = (index >= 256) & (index < 512)
        return index & 63, jnp.where(own, (index & 127) >> 6, 2)

    outer_pairs = pair_forces(
        [
            (*slab, take_pair(*own, pick))
            for slab, pick in ((below, mine[0]), (above, mine[1]))
        ],
        outer,
        index_of,
        code_of,
        lambda: quad_ref[...],
        None,
        outer_work,
    )
    for pairs in (inner_pairs, outer_pairs):
        for _ in range(4):
            next(pairs, None)
    v_ref, _, low_ref, code_ref = work[:4]
    level = levels(64, 256)
    wide = lambda ref, rows: jnp.concatenate([ref[h, rows, :] for h in range(2)], axis=1)
    passed = joined(
        scatter(
            128,
            lambda slot: one_hot(wide(low_ref, pl.ds(slot, 1)), level),
            lambda slot: coded(wide(v_ref, pl.ds(slot * 8, 8)), wide(code_ref, pl.ds(slot, 1)), 4),
        )
    )

    v_ref, _, low_ref, code_ref = outer_work[:4]
    level = levels(64, 128)
    returned = [
        joined(
            scatter(
                128,
                lambda slot, half=half: one_hot(low_ref[half, pl.ds(slot, 1), :], level),
                lambda slot, half=half: coded(
                    v_ref[half, pl.ds(slot * 8, 8), :], code_ref[half, pl.ds(slot, 1), :], 2
                ),
            )
        )
        for half in range(2)
    ]
    own = jnp.concatenate(own, axis=1)
    back = places(own)
    total = grad_ref[...] + jnp.concatenate(returned, axis=1)
    grad = passed + jnp.concatenate(
        [
            take_pair(total[:, 0:128], total[:, 128:256], back[:, h * 128 : h * 128 + 128])
            for h in range(2)
        ],
        axis=1,
    )
    for c in range(3):
        forces_ref[c] = -grad[c * 2 : c * 2 + 2]
    rows = base_rows(own, momenta_ref, noise_ref) + push_rows(grad, own)
    send_ref[...] = dot3(table_ref[...], rows)


WORK = [
    (2, 1024, 128),
    (8, 256),
    (2, 128, 128),
    (2, 128, 128),
    (42, 8, 128),
    (2, 128, 128),
    (4, 128, 128),
    (4, 5, 128, 128),
    (4, 2, 128, 128),
    (4, 32, 128, 128),
    (4, 64, 128),
    (4, 64, 128),
]


def push_rows(grad, own):
    push = grad * -0.25
    mass = jnp.where(own[6:7] > 0.5, 1.0, 16.0)
    none = jnp.zeros((8, 256), F32)
    return halves([none, none, push / mass, push, none, none, none])


def base_rows(own, momenta_ref, noise_ref):
    light = own[6:7] > 0.5
    mass = jnp.where(light, 1.0, 16.0)
    root = jnp.where(light, 1.0, 4.0)
    blank = jnp.zeros((2, 256), F32)
    moment = jnp.concatenate([momenta_ref[c] for c in range(3)] + [blank], axis=0)
    first = jnp.concatenate([noise_ref[c] for c in range(3)] + [blank], axis=0)
    second = jnp.concatenate([noise_ref[3 + c] for c in range(3)] + [blank], axis=0)
    return halves(
        [own, own * mass, moment / mass, moment, first / root, first * root, second * root]
    )


def finish_kernel(parts_ref, positions_ref, momenta_ref):
    total = parts_ref[0]
    for d in range(1, 16):
        total = total + parts_ref[d]
    for half in range(2):
        cols = slice(half * 128, half * 128 + 128)
        for c in range(3):
            row = half * 12 + c * 2
            positions_ref[c, :, cols] = total[row : row + 2]
            momenta_ref[c, :, cols] = total[row + 6 : row + 8]


LIMIT = 62


def call(kernel, shapes, operands, name, mib, fetched=(), scratch=()):
    buffers = [
        pltpu.VMEM(value.shape[1:] if value.shape == STEP_TABLE.shape else value.shape, value.dtype)
        for value in fetched
    ]
    if fetched:
        buffers.append(pltpu.SemaphoreType.DMA((len(fetched),)))
    return pl.pallas_call(
        kernel,
        out_shape=[jax.ShapeDtypeStruct(shape, F32) for shape in shapes],
        in_specs=[WHOLE] * len(operands) + [pl.BlockSpec(memory_space=pl.ANY)] * len(fetched),
        out_specs=[WHOLE] * len(shapes),
        scratch_shapes=buffers + [pltpu.VMEM(shape, F32) for shape in scratch],
        compiler_params=pltpu.CompilerParams(vmem_limit_bytes=mib * 1024 * 1024),
        name=name,
    )(*operands, *fetched)


def per_device(
    positions, momenta, species, neighbours, ghost_index, sparse_points, coefficients, noise
):
    size = lax.axis_size("space")
    close = [(i, i ^ 1) for i in range(size)]
    distant = [(i, (i + 1) % size if i % 2 else (i - 1) % size) for i in range(size)]
    turn = lambda value: jnp.transpose(value, (1, 0, 2))
    own, to_far, to_near = call(
        pack_kernel,
        [(16, 128), (144, 128), (144, 128)],
        (turn(positions), species.reshape(1, 256), ghost_index, neighbours),
        "pack",
        LIMIT,
    )
    far = lax.ppermute(to_far, "space", distant)
    near = lax.ppermute(to_near, "space", close)
    forces, send = call(
        merged_kernel,
        [(3, 2, 256), (384, 128)],
        (),
        "forces",
        LIMIT,
        (own, far, near, neighbours, sparse_points, coefficients, turn(momenta), turn(noise))
        + (jnp.asarray(STEP_TABLE),),
        [(128, 64), (8, 256)] + WORK + WORK,
    )
    parts = lax.all_to_all(send.reshape(16, 24, 128), "bead", split_axis=0, concat_axis=0, tiled=True)
    new_positions, new_momenta = call(finish_kernel, [(3, 2, 256)] * 2, (parts,), "finish", 1)
    return (turn(new_positions), turn(new_momenta), turn(forces))


def solution(mesh):
    placed = (
        P("bead", None, "space"),
        P("bead", None, "space"),
        P("space"),
        P(None, "space"),
        P(None, "space"),
        P(),
        P(),
        P("bead", None, "space"),
    )
    return jax.shard_map(
        per_device,
        mesh=mesh,
        in_specs=placed,
        out_specs=(P("bead", None, "space"), P("bead", None, "space"), P("bead", None, "space")),
        check_vma=False,
    )
```

```python
import functools
import math

import jax
import jax.numpy as jnp
import numpy as np
from jax import lax
from jax.experimental import pallas as pl
from jax.experimental.pallas import tpu as pltpu
from jax.sharding import PartitionSpec as P

BEADS = 32
NRAD = 32
HI = lax.Precision.HIGHEST
F32 = jnp.float32
BF16 = jnp.bfloat16
WHOLE = pl.BlockSpec(memory_space=pltpu.VMEM)


def step_tables():
    index = np.arange(BEADS)
    angle = 2.0 * np.pi * np.outer(index, index) / BEADS
    modes = np.where(
        index == 0,
        1.0 / np.sqrt(BEADS),
        np.where(
            2 * index < BEADS,
            np.sqrt(2.0 / BEADS) * np.cos(angle),
            np.where(
                2 * index == BEADS,
                np.cos(angle) / np.sqrt(BEADS),
                np.sqrt(2.0 / BEADS) * np.sin(angle),
            ),
        ),
    )
    freq = 2.0 * np.sin(np.pi * index / BEADS)
    keep = np.exp(-0.25 * np.where(index == 0, 0.2, 2.0 * freq))
    fresh = np.sqrt(1.0 - keep * keep)
    cosine, sine = np.cos(0.5 * freq), np.sin(0.5 * freq)
    spread = np.where(index == 0, 0.5, sine / np.where(index == 0, 1.0, freq))
    kinds = [
        (0, (modes * cosine) @ modes.T),
        (1, -(modes * (keep * freq * sine)) @ modes.T),
        (0, (modes * (spread * keep)) @ modes.T),
        (1, (modes * (keep * keep * cosine)) @ modes.T),
        (0, modes * (spread * fresh)),
        (1, modes * (keep * cosine * fresh)),
        (1, modes * fresh),
    ]
    base = np.zeros((16, 16, 2, 2, 3, 2, 2, 7, 8))
    for kind, (output, matrix) in enumerate(kinds):
        blocks = matrix.reshape(16, 2, 16, 2)
        for sender in range(16):
            for half in range(2):
                for b in range(2):
                    for c in range(3):
                        base[sender, :, half, output, c, :, half, kind, c * 2 + b] = blocks[
                            :, :, sender, b
                        ]
    return base.reshape(16, 384, 112).astype(np.float32)


STEP_TABLE = step_tables()


def lanes(row, count=8):
    return jnp.broadcast_to(row, (count, 128))


def take(chunk, index):
    return jnp.take_along_axis(chunk, index, axis=1, mode="promise_in_bounds")


def take_pair(low, high, index):
    local = index & 127
    return jnp.where(index < 128, take(low, local), take(high, local))


def halves(pieces):
    return jnp.concatenate([p[:, 0:128] for p in pieces] + [p[:, 128:256] for p in pieces], axis=0)


def fetch(sources, targets, semaphores):
    copies = [
        pltpu.make_async_copy(source, target, semaphores.at[i])
        for i, (source, target) in enumerate(zip(sources, targets))
    ]
    for copy in copies:
        copy.start()
    return copies


def pack_kernel(positions_ref, species_ref, ghost_ref, nbr_ref, own_ref, far_ref, near_ref):
    rows = jnp.concatenate(
        [positions_ref[c] for c in range(3)]
        + [species_ref[...].astype(F32)]
        + [jnp.concatenate([ghost_ref[0:1, :], ghost_ref[1:2, :]], axis=1).astype(F32)],
        axis=0,
    )
    odd = odd_slab()
    low, high = (lanes(ghost_ref[h : h + 1, :]) for h in range(2))
    picks = jnp.where(odd, high, low), jnp.where(odd, low, high)
    for half in range(2):
        block = slice(half * 8, half * 8 + 8)
        part = rows[:, half * 128 : half * 128 + 128]
        own_ref[block, :] = part
        far_ref[block, :] = part
        near_ref[block, :] = part
    for s in range(16):
        block = slice(s * 8, s * 8 + 8)
        left, right = nbr_ref[block, 0:128], nbr_ref[block, 128:256]
        for target, pick in zip((far_ref, near_ref), picks):
            target[16 + s * 8 : 24 + s * 8, :] = take_pair(left, right, pick).astype(F32)


def split(value):
    coarse = value.astype(BF16)
    return coarse, (value - coarse.astype(F32)).astype(BF16)


def dot3(left, right):
    a, b = split(left)
    c, d = split(right)
    dot = functools.partial(jnp.dot, preferred_element_type=F32)
    return dot(a, c) + (dot(a, d) + dot(b, c))


def odd_slab():
    return jnp.full((8, 128), lax.axis_index("space") % 2, jnp.int32) == 1


def column_sums(values):
    row = lax.broadcasted_iota(jnp.int32, (8, 128), 0)
    top = row < 4
    four = [
        jnp.where(top, values[k], values[k + 4])
        + pltpu.roll(jnp.where(top, values[k + 4], values[k]), 4, 0)
        for k in range(4)
    ]
    top = (row & 3) < 2
    two = [
        jnp.where(
            top, four[k] + pltpu.roll(four[k], 6, 0), four[k + 2] + pltpu.roll(four[k + 2], 2, 0)
        )
        for k in range(2)
    ]
    top = (row & 1) < 1
    return jnp.where(top, two[0] + pltpu.roll(two[0], 7, 0), two[1] + pltpu.roll(two[1], 1, 0))


def taps():
    away = (lax.broadcasted_iota(jnp.int32, (8, 128), 0) - 4).astype(F32)
    return jnp.exp(away * away * -0.5)


def quadratic(sparse, weight):
    basis = sparse * lax.rsqrt(jnp.sum(sparse * sparse, axis=0, keepdims=True) + 1e-6)
    scaled = jnp.concatenate([basis * weight[0:1], basis * weight[1:2]], axis=0)
    return lax.dot_general(
        scaled, basis, (((1,), (1,)), ((), ())), precision=HI, preferred_element_type=F32
    )


def places(own):
    same = lax.broadcasted_iota(jnp.int32, (256, 256), 0) == own[7:8].astype(jnp.int32)
    place = lax.broadcasted_iota(jnp.int32, (8, 256), 1).astype(F32).astype(BF16)
    return lax.dot_general(
        place,
        jnp.where(same, 1.0, 0.0).astype(BF16),
        (((1,), (1,)), ((), ())),
        preferred_element_type=F32,
    ).astype(jnp.int32)


def scatter(slots, hot_of, value_of):
    return lax.dot_general(
        jnp.concatenate([hot_of(slot) for slot in range(slots)], axis=1),
        jnp.concatenate([value_of(slot) for slot in range(slots)], axis=1),
        (((1,), (1,)), ((), ())),
        preferred_element_type=F32,
    ).T


def levels(count, wide):
    return lax.broadcasted_iota(jnp.int32, (count, wide), 0).astype(F32).astype(BF16)


def one_hot(row, level):
    count, wide = level.shape
    entry = jnp.broadcast_to(row, (16, wide)).astype(BF16)
    one = jnp.ones((16, wide), BF16)
    return jnp.concatenate(
        [
            jnp.where(entry == level[r * 16 : r * 16 + 16], one, jnp.zeros_like(one))
            for r in range(count // 16)
        ],
        axis=0,
    )


def coded(full, row, codes):
    wide = full.shape[1]
    coarse = full.astype(BF16).astype(F32)
    two = jnp.concatenate([coarse, full - coarse], axis=0).astype(BF16)
    code = jnp.broadcast_to(row, (16, wide)).astype(BF16)
    return jnp.concatenate(
        [
            jnp.where(code == jnp.full((16, wide), c, BF16), two, jnp.zeros_like(two))
            for c in range(codes)
        ],
        axis=0,
    )


def joined(sums):
    grad = jnp.concatenate(
        [sums[c : c + 8] + sums[c + 8 : c + 16] for c in range(0, sums.shape[0], 16)], axis=1
    )
    return jnp.where(lax.broadcasted_iota(jnp.int32, grad.shape, 0) < 6, grad, 0.0)


def pair_forces(chunks, picks, index_of, code_of, quad_of, grad_ref, work):
    (v_ref, central_ref, low_ref, code_ref, src_ref, hyd_ref, t_ref, geo_ref, e_ref, p_ref) = work[:10]
    desc_ref, g_ref = work[10:]
    for half in range(2):
        for c in range(3):
            for r in range(7):
                src_ref[(half * 3 + c) * 7 + r] = lanes(chunks[half][c][r : r + 1])

    for half in range(2):
        cols = slice(half * 128, half * 128 + 128)
        central_ref[:, cols] = take_pair(chunks[half][0], chunks[half][1], picks[half])

        def gather(s, carry, half=half, cols=cols):
            rows = pl.ds(pl.multiple_of(s * 8, 8), 8)
            index = index_of(half, rows)
            local = index & 127
            first = index < 128
            own = index < 256
            live = index < 512
            low, code = code_of(index)
            low_ref[half, rows, :] = low.astype(F32)
            code_ref[half, rows, :] = code.astype(F32)

            def fetch(r):
                found = [take(src_ref[(half * 3 + c) * 7 + r], local) for c in range(3)]
                return jnp.where(own, jnp.where(first, found[0], found[1]), found[2])

            hyd_ref[half, rows, :] = fetch(6)
            for b in range(2):
                bl = b * 2 + half
                delta = [
                    fetch(c * 2 + b) - lanes(central_ref[c * 2 + b : c * 2 + b + 1, cols])
                    for c in range(3)
                ]
                square = delta[0] * delta[0] + delta[1] * delta[1] + delta[2] * delta[2] + 0.25
                inverse = lax.rsqrt(square)
                ratio = square * (1.0 / 25.0)
                keep = jnp.where(live & (ratio < 1.0), 1.0 - ratio, 0.0)
                reach = jnp.minimum(square * inverse * 6.4, 32.0)
                t_ref[bl, rows, :] = reach
                for c in range(3):
                    geo_ref[bl, c, rows, :] = delta[c]
                geo_ref[bl, 3, rows, :] = inverse
                geo_ref[bl, 4, rows, :] = keep
                e_ref[bl, 0, rows, :] = jnp.exp(reach)
                e_ref[bl, 1, rows, :] = jnp.exp(-reach)
            return carry

        lax.fori_loop(0, 16, gather, 0, unroll=16)

    yield
    tap = taps()

    def radial(bl, carry):
        half = bl & 1
        for a in range(4):
            center = 8.0 * a + 4.0

            def step(s, total, center=center, a=a):
                rows = pl.ds(pl.multiple_of(s * 8, 8), 8)
                tau = t_ref[bl, rows, :] - center
                keep = geo_ref[bl, 4, rows, :]
                hydro = hyd_ref[half, rows, :]
                up = e_ref[bl, 0, rows, :] * math.exp(-center)
                down = e_ref[bl, 1, rows, :] * math.exp(center)
                tower = [None] * 8
                tower[4] = jnp.exp(tau * tau * -0.5) * (keep * keep)
                for m in range(5, 8):
                    tower[m] = tower[m - 1] * up
                for m in range(3, -1, -1):
                    tower[m] = tower[m + 1] * down
                new = []
                for m in range(8):
                    p_ref[bl, a * 8 + m, rows, :] = tower[m]
                    new.append(total[2 * m] + tower[m])
                    new.append(total[2 * m + 1] + tower[m] * hydro)
                return tuple(new)

            zero = jnp.zeros((8, 128), F32)
            total = lax.fori_loop(0, 16, step, (zero,) * 16, unroll=16)
            every = column_sums(total[0::2])
            hydrogen = column_sums(total[1::2])
            desc_ref[bl, a * 8 : a * 8 + 8, :] = (every - hydrogen) * tap
            desc_ref[bl, NRAD + a * 8 : NRAD + a * 8 + 8, :] = hydrogen * tap
        return carry

    lax.fori_loop(0, 4, radial, 0, unroll=4)

    yield
    desc = [desc_ref[bl] for bl in range(4)]
    norm = [lax.rsqrt(jnp.sum(d * d, axis=0, keepdims=True) + 1e-6) for d in desc]
    unit = [d * n for d, n in zip(desc, norm)]
    turned = dot3(quad_of(), jnp.concatenate(unit, axis=1))
    tap = jnp.concatenate([taps()] * 8, axis=0)
    for bl in range(4):
        half = bl & 1
        heavy = central_ref[6:7, half * 128 : half * 128 + 128] < 0.5
        mine = turned[:, bl * 128 : bl * 128 + 128]
        slope = jnp.where(heavy, mine[0:64], mine[64:128])
        along = jnp.sum(slope * unit[bl], axis=0, keepdims=True)
        g_ref[bl] = (2.0 * norm[bl]) * (slope - unit[bl] * along) * tap

    yield
    group = 4
    if grad_ref is not None:
        grad_ref[6:8, :] = jnp.zeros((2, 256), F32)
    for b in range(2):
        for half in range(2):
            bl = b * 2 + half

            def back(s, total, b=b, bl=bl, half=half):
                start = pl.multiple_of(s * (8 * group), 8 * group)
                rows = [pl.ds(start + 8 * q, 8) for q in range(group)]
                hydro = [hyd_ref[half, r, :] > 0.5 for r in rows]
                plain = [None] * group
                ramp = [None] * group
                for k in range(NRAD - 1, -1, -1):
                    oxygen = lanes(g_ref[bl, k : k + 1, :])
                    hydrogen = lanes(g_ref[bl, NRAD + k : NRAD + k + 1, :])
                    for q in range(group):
                        x = p_ref[bl, k, rows[q], :] * jnp.where(hydro[q], hydrogen, oxygen)
                        plain[q] = x if k == NRAD - 1 else plain[q] + x
                        ramp[q] = plain[q] if k == NRAD - 1 else ramp[q] + plain[q]
                total = list(total)
                for q in range(group):
                    reach = t_ref[bl, rows[q], :]
                    inverse = geo_ref[bl, 3, rows[q], :]
                    keep = geo_ref[bl, 4, rows[q], :]
                    inside = keep > 0.0
                    fade = jnp.where(inside, (-4.0 / 25.0) / jnp.where(inside, keep, 1.0), 0.0)
                    slope = (reach + 1.0) * plain[q] - ramp[q]
                    pull = plain[q] * fade - 6.4 * slope * inverse
                    for c in range(3):
                        part = pull * geo_ref[bl, c, rows[q], :]
                        total[c] = total[c] + part
                        v_ref[half, pl.ds((start + 8 * q) * 8 + c * 2 + b, 8, stride=8), :] = part
                return tuple(total)

            zero = jnp.zeros((8, 128), F32)
            total = lax.fori_loop(0, 16 // group, back, (zero,) * 3, unroll=4)
            for c in range(3):
                if grad_ref is not None:
                    grad_ref[c * 2 + b : c * 2 + b + 1, half * 128 : half * 128 + 128] = -jnp.sum(
                        total[c], axis=0, keepdims=True
                    )


def merged_kernel(
    own_hbm,
    far_hbm,
    near_hbm,
    nbr_hbm,
    sparse_hbm,
    coef_hbm,
    momenta_hbm,
    noise_hbm,
    tables_hbm,
    forces_ref,
    send_ref,
    own_ref,
    far_ref,
    near_ref,
    nbr_ref,
    sparse_ref,
    coef_ref,
    momenta_ref,
    noise_ref,
    table_ref,
    sems,
    quad_ref,
    grad_ref,
    *work,
):
    work, outer_work = work[: len(WORK)], work[len(WORK) :]
    copies = fetch(
        (own_hbm, far_hbm, near_hbm, nbr_hbm, sparse_hbm, coef_hbm, momenta_hbm, noise_hbm)
        + (tables_hbm.at[lax.axis_index("bead")],),
        (own_ref, far_ref, near_ref, nbr_ref, sparse_ref, coef_ref, momenta_ref, noise_ref)
        + (table_ref,),
        sems,
    )
    for copy in copies[:4]:
        copy.wait()
    odd = odd_slab()
    chunk = lambda ref, h: ref[h * 8 : h * 8 + 8, :]
    own = [chunk(own_ref, h) for h in range(2)]
    far = [chunk(far_ref, h) for h in range(2)]
    near = [chunk(near_ref, h) for h in range(2)]
    below = [jnp.where(odd, n, f) for f, n in zip(far, near)]
    above = [jnp.where(odd, f, n) for f, n in zip(far, near)]
    listed = lambda slab, h: lanes(slab[h][7:8]).astype(jnp.int32)

    def quad_of():
        for copy in copies[4:]:
            copy.wait()
        quad_ref[...] = quadratic(sparse_ref[...], coef_ref[...])
        return quad_ref[...]

    mine = [listed(own, h) for h in range(2)]
    outer = [listed(below, 1), listed(above, 0)]
    copied = [take_pair(*below, outer[0]), take_pair(*above, outer[1])]
    inner_pairs = pair_forces(
        [(*own, copied[h]) for h in range(2)],
        mine,
        lambda half, rows: take_pair(nbr_ref[rows, 0:128], nbr_ref[rows, 128:256], mine[half]),
        lambda index: (index & 63, index >> 6),
        quad_of,
        grad_ref,
        work,
    )
    def index_of(half, rows):
        there = pl.ds(16 + rows.start, rows.size)
        f, n = far_ref[there, :], near_ref[there, :]
        found = jnp.where(odd, n, f) if half == 0 else jnp.where(odd, f, n)
        return found.astype(jnp.int32)

    def code_of(index):
        own = (index >= 256) & (index < 512)
        return index & 63, jnp.where(own, (index & 127) >> 6, 2)

    outer_pairs = pair_forces(
        [
            (*slab, take_pair(*own, pick))
            for slab, pick in ((below, mine[0]), (above, mine[1]))
        ],
        outer,
        index_of,
        code_of,
        lambda: quad_ref[...],
        None,
        outer_work,
    )
    for pairs in (inner_pairs, outer_pairs):
        for _ in range(4):
            next(pairs, None)
    v_ref, _, low_ref, code_ref = work[:4]
    level = levels(64, 256)
    wide = lambda ref, rows: jnp.concatenate([ref[h, rows, :] for h in range(2)], axis=1)
    passed = joined(
        scatter(
            128,
            lambda slot: one_hot(wide(low_ref, pl.ds(slot, 1)), level),
            lambda slot: coded(wide(v_ref, pl.ds(slot * 8, 8)), wide(code_ref, pl.ds(slot, 1)), 4),
        )
    )

    v_ref, _, low_ref, code_ref = outer_work[:4]
    level = levels(64, 128)
    returned = [
        joined(
            scatter(
                128,
                lambda slot, half=half: one_hot(low_ref[half, pl.ds(slot, 1), :], level),
                lambda slot, half=half: coded(
                    v_ref[half, pl.ds(slot * 8, 8), :], code_ref[half, pl.ds(slot, 1), :], 2
                ),
            )
        )
        for half in range(2)
    ]
    own = jnp.concatenate(own, axis=1)
    back = places(own)
    total = grad_ref[...] + jnp.concatenate(returned, axis=1)
    grad = passed + jnp.concatenate(
        [
            take_pair(total[:, 0:128], total[:, 128:256], back[:, h * 128 : h * 128 + 128])
            for h in range(2)
        ],
        axis=1,
    )
    for c in range(3):
        forces_ref[c] = -grad[c * 2 : c * 2 + 2]
    rows = base_rows(own, momenta_ref, noise_ref) + push_rows(grad, own)
    send_ref[...] = dot3(table_ref[...], rows)


WORK = [
    (2, 1032, 128),
    (8, 256),
    (2, 128, 128),
    (2, 128, 128),
    (42, 8, 128),
    (2, 128, 128),
    (4, 128, 128),
    (4, 5, 128, 128),
    (4, 2, 128, 128),
    (4, 32, 128, 128),
    (4, 64, 128),
    (4, 64, 128),
]


def push_rows(grad, own):
    push = grad * -0.25
    mass = jnp.where(own[6:7] > 0.5, 1.0, 16.0)
    none = jnp.zeros((8, 256), F32)
    return halves([none, none, push / mass, push, none, none, none])


def base_rows(own, momenta_ref, noise_ref):
    light = own[6:7] > 0.5
    mass = jnp.where(light, 1.0, 16.0)
    root = jnp.where(light, 1.0, 4.0)
    blank = jnp.zeros((2, 256), F32)
    moment = jnp.concatenate([momenta_ref[c] for c in range(3)] + [blank], axis=0)
    first = jnp.concatenate([noise_ref[c] for c in range(3)] + [blank], axis=0)
    second = jnp.concatenate([noise_ref[3 + c] for c in range(3)] + [blank], axis=0)
    return halves(
        [own, own * mass, moment / mass, moment, first / root, first * root, second * root]
    )


def finish_kernel(parts_ref, positions_ref, momenta_ref):
    total = parts_ref[0]
    for d in range(1, 16):
        total = total + parts_ref[d]
    for half in range(2):
        cols = slice(half * 128, half * 128 + 128)
        for c in range(3):
            row = half * 12 + c * 2
            positions_ref[c, :, cols] = total[row : row + 2]
            momenta_ref[c, :, cols] = total[row + 6 : row + 8]


LIMIT = 62


def call(kernel, shapes, operands, name, mib, fetched=(), scratch=()):
    buffers = [
        pltpu.VMEM(value.shape[1:] if value.shape == STEP_TABLE.shape else value.shape, value.dtype)
        for value in fetched
    ]
    if fetched:
        buffers.append(pltpu.SemaphoreType.DMA((len(fetched),)))
    return pl.pallas_call(
        kernel,
        out_shape=[jax.ShapeDtypeStruct(shape, F32) for shape in shapes],
        in_specs=[WHOLE] * len(operands) + [pl.BlockSpec(memory_space=pl.ANY)] * len(fetched),
        out_specs=[WHOLE] * len(shapes),
        scratch_shapes=buffers + [pltpu.VMEM(shape, F32) for shape in scratch],
        compiler_params=pltpu.CompilerParams(vmem_limit_bytes=mib * 1024 * 1024),
        name=name,
    )(*operands, *fetched)


def per_device(
    positions, momenta, species, neighbours, ghost_index, sparse_points, coefficients, noise
):
    size = lax.axis_size("space")
    close = [(i, i ^ 1) for i in range(size)]
    distant = [(i, (i + 1) % size if i % 2 else (i - 1) % size) for i in range(size)]
    turn = lambda value: jnp.transpose(value, (1, 0, 2))
    own, to_far, to_near = call(
        pack_kernel,
        [(16, 128), (144, 128), (144, 128)],
        (turn(positions), species.reshape(1, 256), ghost_index, neighbours),
        "pack",
        LIMIT,
    )
    far = lax.ppermute(to_far, "space", distant)
    near = lax.ppermute(to_near, "space", close)
    forces, send = call(
        merged_kernel,
        [(3, 2, 256), (384, 128)],
        (),
        "forces",
        LIMIT,
        (own, far, near, neighbours, sparse_points, coefficients, turn(momenta), turn(noise))
        + (jnp.asarray(STEP_TABLE),),
        [(128, 64), (8, 256)] + WORK + WORK,
    )
    parts = lax.all_to_all(send.reshape(16, 24, 128), "bead", split_axis=0, concat_axis=0, tiled=True)
    new_positions, new_momenta = call(finish_kernel, [(3, 2, 256)] * 2, (parts,), "finish", 1)
    return (turn(new_positions), turn(new_momenta), turn(forces))


def solution(mesh):
    placed = (
        P("bead", None, "space"),
        P("bead", None, "space"),
        P("space"),
        P(None, "space"),
        P(None, "space"),
        P(),
        P(),
        P("bead", None, "space"),
    )
    return jax.shard_map(
        per_device,
        mesh=mesh,
        in_specs=placed,
        out_specs=(P("bead", None, "space"), P("bead", None, "space"), P("bead", None, "space")),
        check_vma=False,
    )
```
